256 devices in a mesh: tensor: 8 (over z_hi, y), seq: 32 (over x, z_lo, core).
Axes of the slice: x: 4, y: 4, z: 8 (z_hi: 2, z_lo: 4; z = z_hi * 4 + z_lo), core: 2. Of those that a mesh axis runs over, the one named last changes fastest.
Arguments:
- queries: bfloat16 [16, 524288], P('tensor', 'seq'), may hold values from -6 to 6
- key_feats: bfloat16 [16, 524288], P('tensor', 'seq'), may hold values from -6 to 6
- value_feats: bfloat16 [16, 524288], P('tensor', 'seq'), may hold values from -6 to 6
- filter_taps: bfloat16 [16, 524288], P('tensor', 'seq'), may hold values from -1 to 1
- skip_gain: float32 [16], P('tensor'), may hold values from -4 to 4
- out_weight: bfloat16 [16, 16], replicated, may hold values from -1.5 to 1.5
- out_grad: bfloat16 [16, 524288], P('tensor', 'seq'), may hold values from -6 to 6
Outputs:
- output: bfloat16 [16, 524288], P('tensor', 'seq')
- grad_queries: bfloat16 [16, 524288], P('tensor', 'seq')
- grad_keys: bfloat16 [16, 524288], P('tensor', 'seq')
- grad_values: bfloat16 [16, 524288], P('tensor', 'seq')
- grad_taps: float32 [16, 524288], P('tensor', 'seq')
The draws below stay inside these ranges and needn't reach their ends.
All inputs are finite; a program needn't handle non-finite values.
Results may differ from the reference program's by a relative error of at most 0.015.
Values may be sent and summed in bfloat16 or wider, within the bound.
No kernel may reach another device: no remote copies, remote signals or barrier semaphores. Data moves between devices by JAX's collectives and lax.ppermute only.
A program may use at most 128 MiB of HBM per device.

```python
import math
import jax
import jax.numpy as jnp

CHANNELS = 16
TOKENS = 524288


def draw_filter_taps(key, part):
    key = jax.random.fold_in(key, 7)
    rate_key = jax.random.fold_in(key, 1)
    noise_key = jax.random.fold_in(key, 2)
    timescale = jnp.exp(jax.random.uniform(rate_key, (CHANNELS, 1), jnp.float32, math.log(40.0), math.log(TOKENS * 4.0)))
    noise = jnp.clip(jax.random.normal(noise_key, (CHANNELS, TOKENS), jnp.float32), -4.0, 4.0)
    lags = jnp.arange(TOKENS, dtype=jnp.float32)[None, :]
    taps = noise * jnp.sqrt(2.0 / timescale) * jnp.exp(-lags / timescale)
    return taps.astype(jnp.bfloat16)


def block_levels(stream_key, dims, pieces, smallest, largest):
    loudness = 1.0
    for dim, parts in pieces:
        heights = jax.random.uniform(jax.random.fold_in(jax.random.fold_in(stream_key, 6), dim), (parts,), jnp.float32, smallest / len(pieces), largest / len(pieces))
        loudness = loudness * jnp.repeat(jnp.exp(heights), dims[dim] // parts).reshape((-1,) + (1,) * (len(dims) - 1 - dim))
    return loudness


def gaussian(stream_key, shape, deviation, bound, shards=(), kind=jnp.bfloat16):
    result = deviation * jax.random.normal(stream_key, shape, jnp.float32)
    if shards:
        result = result * block_levels(stream_key, shape, shards, -0.22, 0.18)
    return jnp.clip(result, -bound, bound).astype(kind)


def setup_inputs(seed: int = 0) -> dict:
    seeds = jax.random.split(jax.random.key(seed), 8)
    queries = gaussian(seeds[0], (CHANNELS, TOKENS), 1.0, 6.0, ((0, 8), (1, 32)))
    key_feats = gaussian(seeds[1], (CHANNELS, TOKENS), 1.0, 6.0, ((0, 8), (1, 32)))
    value_feats = gaussian(seeds[2], (CHANNELS, TOKENS), 1.0, 6.0, ((0, 8), (1, 32)))
    filter_taps = draw_filter_taps(jax.random.fold_in(seeds[7], 71), 0)
    skip_gain = gaussian(seeds[4], (CHANNELS,), 1.0, 4.0, ((0, 8),), jnp.float32)
    out_weight = gaussian(seeds[5], (CHANNELS, CHANNELS), CHANNELS ** -0.5, 1.5)
    out_grad = gaussian(seeds[6], (CHANNELS, TOKENS), 1.0, 6.0, ((0, 8), (1, 32)))
    return {"queries": queries, "key_feats": key_feats, "value_feats": value_feats, "filter_taps": filter_taps, "skip_gain": skip_gain, "out_weight": out_weight, "out_grad": out_grad}


def reference(queries, key_feats, value_feats, filter_taps, skip_gain, out_weight, out_grad):
    length = 2 * TOKENS
    key_float = key_feats.astype(jnp.float32)
    value_float = value_feats.astype(jnp.float32)
    query_float = queries.astype(jnp.float32)
    key_value = (key_float * value_float).astype(jnp.bfloat16)
    source = key_value.astype(jnp.float32)
    source_spec = jnp.fft.rfft(source, n=length, axis=1)
    taps_spec = jnp.fft.rfft(filter_taps.astype(jnp.float32), n=length, axis=1)
    convolved = jnp.fft.irfft(source_spec * taps_spec, n=length, axis=1)[:, :TOKENS]
    inner_sum = convolved + skip_gain[:, None] * source
    gated_out = (query_float * inner_sum).astype(jnp.bfloat16)
    output = jnp.dot(out_weight.T, gated_out, preferred_element_type=jnp.float32).astype(jnp.bfloat16)
    grad_gated = jnp.dot(out_weight, out_grad, preferred_element_type=jnp.float32)
    grad_queries = (grad_gated * inner_sum).astype(jnp.bfloat16)
    grad_inner = (grad_gated * query_float).astype(jnp.bfloat16)
    inner_float = grad_inner.astype(jnp.float32)
    grad_spec = jnp.fft.rfft(inner_float, n=length, axis=1)
    grad_source = jnp.fft.irfft(grad_spec * jnp.conj(taps_spec), n=length, axis=1)[:, :TOKENS]
    grad_source = grad_source + skip_gain[:, None] * inner_float
    grad_taps = jnp.fft.irfft(grad_spec * jnp.conj(source_spec), n=length, axis=1)[:, :TOKENS]
    grad_taps = (grad_taps * (TOKENS ** -0.5)).astype(jnp.float32)
    grad_keys = (grad_source * value_float).astype(jnp.bfloat16)
    grad_values = (grad_source * key_float).astype(jnp.bfloat16)
    return output, grad_queries, grad_keys, grad_values, grad_taps
```

```python
import math

import jax
import jax.numpy as jnp
import numpy as np
from jax import lax
from jax.experimental import pallas as pl
from jax.experimental.pallas import tpu as pltpu
from jax.sharding import PartitionSpec as P

F32 = jnp.float32
BF16 = jnp.bfloat16
CH = 2
GROUP = 8
BLOCKS = 32
SIDE = 128
ROWS = CH * SIDE
BLOCK = SIDE * SIDE
LENGTH = 2 * BLOCK
FREQ_ROWS = SIDE // BLOCKS
PIECE = CH * FREQ_ROWS
VMEM = pl.BlockSpec(memory_space=pltpu.VMEM)
SMEM = pl.BlockSpec(memory_space=pltpu.SMEM)
PARAMS = pltpu.CompilerParams(vmem_limit_bytes=48 * 1024 * 1024)


def tables():
    side = np.arange(SIDE)
    k1 = np.arange(BLOCKS)[:, None, None] * FREQ_ROWS + np.arange(FREQ_ROWS)[None, None, :]
    k1 = np.broadcast_to(k1, (BLOCKS, CH, FREQ_ROWS)).reshape(-1)
    chan = np.broadcast_to(np.arange(CH)[None, :, None], (BLOCKS, CH, FREQ_ROWS)).reshape(-1)
    angle = 2 * np.pi * (k1[:, None] + 0.5) * side[None, :] / (2 * SIDE)
    first = np.zeros((2, ROWS, CH, SIDE))
    for c in range(CH):
        mine = (chan == c)[:, None]
        first[0, :, c] = np.where(mine, np.cos(angle), 0)
        first[1, :, c] = np.where(mine, -np.sin(angle), 0)
    first = first.reshape(2 * ROWS, ROWS)
    turn = 2 * np.pi * (k1[:, None] + 0.5) * side[None, :] / LENGTH
    turn = np.stack([np.cos(turn), np.sin(turn)])
    phase = 2 * np.pi * side[:, None] * side[None, :] / SIDE
    second = np.block([[np.cos(phase), -np.sin(phase)], [np.sin(phase), np.cos(phase)]])
    return (
        jnp.asarray(first, BF16),
        jnp.asarray(first.T, BF16),
        jnp.asarray(turn, F32),
        jnp.asarray(second, BF16),
        jnp.asarray(second.T, BF16),
    )


def square(ref):
    return ref[...].astype(F32).reshape(ROWS, SIDE)


def forward(signal, first, turn, second):
    stage = jnp.dot(first, signal, preferred_element_type=F32)
    real, imag = stage[:ROWS], stage[ROWS:]
    cos, sin = turn[0], turn[1]
    turned = jnp.concatenate(
        [(real * cos + imag * sin).astype(BF16), (imag * cos - real * sin).astype(BF16)], axis=1
    )
    spec = jnp.dot(turned, second, preferred_element_type=F32)
    return spec[:, :SIDE], spec[:, SIDE:]


def pack(real, imag):
    both = jnp.concatenate(
        [real.reshape(BLOCKS, PIECE, SIDE), imag.reshape(BLOCKS, PIECE, SIDE)], axis=1
    )
    return both.astype(BF16)


def inverse(rows, first_t, turn, second_t):
    rows = rows.astype(F32)
    real = rows[:, :PIECE].reshape(ROWS, SIDE)
    imag = rows[:, PIECE:].reshape(ROWS, SIDE)
    spec = jnp.concatenate([real.astype(BF16), imag.astype(BF16)], axis=1)
    stage = jnp.dot(spec, second_t, preferred_element_type=F32)
    real, imag = stage[:, :SIDE], stage[:, SIDE:]
    cos, sin = turn[0], turn[1]
    turned = jnp.concatenate(
        [(real * cos - imag * sin).astype(BF16), (imag * cos + real * sin).astype(BF16)], axis=0
    )
    return jnp.dot(first_t, turned, preferred_element_type=F32) * (2.0 / LENGTH)


def spread_kernel(grad_ref, out_ref):
    rows = square(grad_ref).astype(BF16)
    for peer in range(GROUP):
        out_ref[peer] = rows


def source_kernel(key_ref, value_ref, taps_ref, first_ref, turn_ref, second_ref, kv_ref, spec_ref):
    tables_in = (first_ref[...], turn_ref[...], second_ref[...])
    key_value = (square(key_ref) * square(value_ref)).astype(BF16)
    kv_ref[...] = key_value
    spec_ref[:, :16, :] = pack(*forward(key_value, *tables_in))
    spec_ref[:, 16:, :] = pack(*forward(square(taps_ref).astype(BF16), *tables_in))


def mix(weight_ref, all_ref, chan):
    total = None
    for peer in range(GROUP):
        for c in range(CH):
            part = weight_ref[chan, peer * CH + c] * all_ref[
                peer, c * SIDE : (c + 1) * SIDE, :
            ].astype(F32)
            total = part if total is None else total + part
    return total


def grad_kernel(
    weight_ref, grads_ref, query_ref, spec_ref, first_ref, turn_ref, second_ref,
    gated_ref, inner_ref, out_ref,
):
    grad_gated = jnp.concatenate([mix(weight_ref, grads_ref, c) for c in range(CH)], axis=0)
    gated_ref[...] = grad_gated
    grad_inner = (grad_gated * square(query_ref)).astype(BF16)
    inner_ref[...] = grad_inner
    out_ref[:, :32, :] = spec_ref[...]
    out_ref[:, 32:, :] = pack(
        *forward(grad_inner, first_ref[...], turn_ref[...], second_ref[...])
    )


def block_kernel(spec_ref, out_ref, buf_ref):
    for sig in range(3):
        both = spec_ref[:, 16 * sig : 16 * sig + 16, :].astype(F32)
        buf_ref[sig, 0] = both[:, :PIECE]
        buf_ref[sig, 1] = both[:, PIECE:]
    row = lax.broadcasted_iota(jnp.int32, (PIECE, SIDE), 0)
    sign = jnp.where(row % 2 == 0, 1.0, -1.0).astype(F32)
    source, taps, grad = 0, 1, 2
    tile = 4

    def at(sig, blk):
        return buf_ref[sig, 0, blk], buf_ref[sig, 1, blk]

    def put(sig, blk, real, imag):
        out_ref[blk, 16 * sig : 16 * sig + 16, :] = jnp.concatenate([real, imag], axis=0).astype(
            BF16
        )

    def add(total, real, imag):
        return (real, imag) if total is None else (total[0] + real, total[1] + imag)

    last = None
    for base in range(0, BLOCKS, tile):
        sums = [None] * tile
        window = {}
        for j in range(base + tile):
            hr, hi = at(taps, j)
            for o in range(tile):
                blk = base + o - j
                if blk < 0:
                    continue
                if blk not in window:
                    window[blk] = at(source, blk)
                xr, xi = window[blk]
                sums[o] = add(sums[o], hr * xr - hi * xi, hr * xi + hi * xr)
        for o in range(tile):
            real, imag = sums[o]
            if last is not None:
                real, imag = real - sign * last[1], imag + sign * last[0]
            put(0, base + o, real, imag)
            last = sums[o]

    for slot, other in ((1, taps), (2, source)):
        after = None
        for base in range(BLOCKS - tile, -1, -tile):
            sums = [None] * tile
            window = {}
            for j in range(BLOCKS - base):
                hr, hi = at(other, j)
                for o in range(tile):
                    blk = base + o + j
                    if blk >= BLOCKS:
                        continue
                    if blk not in window:
                        window[blk] = at(grad, blk)
                    gr, gi = window[blk]
                    sums[o] = add(sums[o], gr * hr + gi * hi, gi * hr - gr * hi)
            for o in range(tile - 1, -1, -1):
                real, imag = sums[o]
                if after is not None:
                    real, imag = real + sign * after[1], imag - sign * after[0]
                put(slot, base + o, real, imag)
                after = sums[o]


def gate_kernel(
    skip_ref, rows_ref, kv_ref, query_ref, gated_ref, first_ref, turn_ref, second_ref,
    spread_ref, grad_query_ref,
):
    convolved = inverse(rows_ref[:, :16, :], first_ref[...], turn_ref[...], second_ref[...])
    inner_sum = convolved + skip_rows(skip_ref) * kv_ref[...].astype(F32)
    gated = (square(query_ref) * inner_sum).astype(BF16)
    for peer in range(GROUP):
        spread_ref[peer] = gated
    grad_query_ref[...] = (gated_ref[...] * inner_sum).reshape(CH, BLOCK).astype(BF16)


def skip_rows(skip_ref):
    row = lax.broadcasted_iota(jnp.int32, (ROWS, SIDE), 0)
    return jnp.where(row < SIDE, skip_ref[0], skip_ref[1])


def grads_kernel(
    skip_ref, rows_ref, inner_ref, key_ref, value_ref, first_ref, turn_ref, second_ref,
    grad_key_ref, grad_value_ref, grad_taps_ref, *, scale,
):
    tables_in = (first_ref[...], turn_ref[...], second_ref[...])
    source = inverse(rows_ref[:, 16:32, :], *tables_in)
    source = source + skip_rows(skip_ref) * inner_ref[...].astype(F32)
    source = source.reshape(CH, BLOCK)
    grad_key_ref[...] = (source * value_ref[...].astype(F32)).astype(BF16)
    grad_value_ref[...] = (source * key_ref[...].astype(F32)).astype(BF16)
    taps = inverse(rows_ref[:, 32:, :], *tables_in) * scale
    grad_taps_ref[...] = taps.reshape(CH, BLOCK)


def output_kernel(weight_ref, all_ref, out_ref):
    both = jnp.concatenate([mix(weight_ref, all_ref, c) for c in range(CH)], axis=0)
    out_ref[...] = both.reshape(CH, BLOCK).astype(BF16)


def call(kernel, outs, operands, smem=0, scratch=()):
    return pl.pallas_call(
        kernel,
        out_shape=[jax.ShapeDtypeStruct(shape, dtype) for shape, dtype in outs],
        in_specs=[SMEM] * smem + [VMEM] * (len(operands) - smem),
        out_specs=[VMEM] * len(outs),
        scratch_shapes=list(scratch),
        compiler_params=PARAMS,
    )(*operands)


def exchange(blocks, axis):
    return lax.all_to_all(blocks, axis, split_axis=0, concat_axis=0, tiled=True)


def body(queries, key_feats, value_feats, filter_taps, skip_gain, out_weight, out_grad):
    first, first_t, turn, second, second_t = tables()
    forward_tables = (first, turn, second)
    inverse_tables = (first_t, turn, second_t)
    start = lax.axis_index("tensor") * CH
    weight = out_weight.astype(F32)
    weight_rows = lax.dynamic_slice_in_dim(weight, start, CH, 0)
    weight_cols = lax.dynamic_slice_in_dim(weight, start, CH, 1).T
    square_shape = (ROWS, SIDE)
    spread_shape = (GROUP, ROWS, SIDE)
    tokens = (CH, BLOCK)

    (spread,) = call(spread_kernel, [(spread_shape, BF16)], (out_grad,))
    all_grads = exchange(spread, "tensor")
    key_value, spec = call(
        source_kernel,
        [(square_shape, BF16), ((BLOCKS, 32, SIDE), BF16)],
        (key_feats, value_feats, filter_taps, *forward_tables),
    )
    grad_gated, grad_inner, spec = call(
        grad_kernel,
        [(square_shape, F32), (square_shape, BF16), ((BLOCKS, 48, SIDE), BF16)],
        (weight_rows, all_grads, queries, spec, *forward_tables),
        smem=1,
    )
    spec = exchange(spec, "seq")
    (rows,) = call(
        block_kernel,
        [((BLOCKS, 48, SIDE), BF16)],
        (spec,),
        scratch=[pltpu.VMEM((3, 2, BLOCKS, PIECE, SIDE), F32)],
    )
    rows = exchange(rows, "seq")
    spread, grad_queries = call(
        gate_kernel,
        [(spread_shape, BF16), (tokens, BF16)],
        (skip_gain, rows, key_value, queries, grad_gated, *inverse_tables),
        smem=1,
    )
    all_gated = exchange(spread, "tensor")

    def grads(*refs):
        grads_kernel(*refs, scale=(BLOCKS * BLOCK) ** -0.5)

    grad_keys, grad_values, grad_taps = call(
        grads,
        [(tokens, BF16), (tokens, BF16), (tokens, F32)],
        (skip_gain, rows, grad_inner, key_feats, value_feats, *inverse_tables),
        smem=1,
    )
    (output,) = call(output_kernel, [(tokens, BF16)], (weight_cols, all_gated), smem=1)
    return (output, grad_queries, grad_keys, grad_values, grad_taps)


def solution(mesh):
    assert dict(mesh.shape) == {"tensor": GROUP, "seq": BLOCKS}
    placed = P("tensor", "seq")
    return jax.shard_map(
        body,
        mesh=mesh,
        in_specs=(placed, placed, placed, placed, P("tensor"), P(), placed),
        out_specs=(placed,) * 5,
        check_vma=False,
    )
```

```python
import math

import jax
import jax.numpy as jnp
import numpy as np
from jax import lax
from jax.experimental import pallas as pl
from jax.experimental.pallas import tpu as pltpu
from jax.sharding import PartitionSpec as P

F32 = jnp.float32
BF16 = jnp.bfloat16
CH = 2
GROUP = 8
RING = 4
TILE = 4
BLOCKS = 32
SIDE = 128
ROWS = CH * SIDE
BLOCK = SIDE * SIDE
LENGTH = 2 * BLOCK
FREQ_ROWS = SIDE // BLOCKS
PIECE = CH * FREQ_ROWS
VMEM = pl.BlockSpec(memory_space=pltpu.VMEM)
SMEM = pl.BlockSpec(memory_space=pltpu.SMEM)
HBM = pl.BlockSpec(memory_space=pltpu.HBM)


def tables():
    side = np.arange(SIDE)
    k1 = np.arange(BLOCKS)[:, None, None] * FREQ_ROWS + np.arange(FREQ_ROWS)[None, None, :]
    k1 = np.broadcast_to(k1, (BLOCKS, CH, FREQ_ROWS)).reshape(-1)
    chan = np.broadcast_to(np.arange(CH)[None, :, None], (BLOCKS, CH, FREQ_ROWS)).reshape(-1)
    angle = 2 * np.pi * (k1[:, None] + 0.5) * side[None, :] / (2 * SIDE)
    first = np.zeros((2, ROWS, CH, SIDE))
    for c in range(CH):
        mine = (chan == c)[:, None]
        first[0, :, c] = np.where(mine, np.cos(angle), 0)
        first[1, :, c] = np.where(mine, -np.sin(angle), 0)
    first = first.reshape(2 * ROWS, ROWS)
    turn = 2 * np.pi * (k1[:, None] + 0.5) * side[None, :] / LENGTH
    turn = np.stack([np.cos(turn), np.sin(turn)])
    phase = 2 * np.pi * side[:, None] * side[None, :] / SIDE
    second = np.block([[np.cos(phase), -np.sin(phase)], [np.sin(phase), np.cos(phase)]])
    return (
        jnp.asarray(first, BF16),
        jnp.asarray(first.T, BF16),
        jnp.asarray(turn, F32),
        jnp.asarray(second, BF16),
        jnp.asarray(second.T, BF16),
    )


def square(ref):
    return ref[...].astype(F32).reshape(ROWS, SIDE)


def forward(signal, first, turn, second):
    stage = jnp.dot(first, signal, preferred_element_type=F32)
    real, imag = stage[:ROWS], stage[ROWS:]
    cos, sin = turn[0], turn[1]
    turned = jnp.concatenate(
        [(real * cos + imag * sin).astype(BF16), (imag * cos - real * sin).astype(BF16)], axis=1
    )
    spec = jnp.dot(turned, second, preferred_element_type=F32)
    return spec[:, :SIDE], spec[:, SIDE:]


def pack(real, imag):
    both = jnp.concatenate(
        [real.reshape(BLOCKS, PIECE, SIDE), imag.reshape(BLOCKS, PIECE, SIDE)], axis=1
    )
    return both.astype(BF16)


def inverse(rows, first_t, turn, second_t):
    rows = rows.astype(F32)
    real = rows[:, :PIECE].reshape(ROWS, SIDE)
    imag = rows[:, PIECE:].reshape(ROWS, SIDE)
    spec = jnp.concatenate([real.astype(BF16), imag.astype(BF16)], axis=1)
    stage = jnp.dot(spec, second_t, preferred_element_type=F32)
    real, imag = stage[:, :SIDE], stage[:, SIDE:]
    cos, sin = turn[0], turn[1]
    turned = jnp.concatenate(
        [(real * cos - imag * sin).astype(BF16), (imag * cos + real * sin).astype(BF16)], axis=0
    )
    return jnp.dot(first_t, turned, preferred_element_type=F32) * (2.0 / LENGTH)


def source_kernel(
    key_hbm, value_hbm, taps_hbm, first_hbm, turn_hbm, second_hbm, kv_ref, spec_ref,
    key_ref, value_ref, taps_ref, first_ref, turn_ref, second_ref, sems,
):
    pairs = (
        (key_hbm, key_ref),
        (value_hbm, value_ref),
        (taps_hbm, taps_ref),
        (first_hbm, first_ref),
        (turn_hbm, turn_ref),
        (second_hbm, second_ref),
    )
    copies = [
        pltpu.make_async_copy(src, dst, sems.at[i]) for i, (src, dst) in enumerate(pairs)
    ]
    for copy in copies:
        copy.start()
    for copy in copies:
        copy.wait()
    tables_in = (first_ref[...], turn_ref[...], second_ref[...])
    key_value = (square(key_ref) * square(value_ref)).astype(BF16)
    kv_ref[...] = key_value
    spec_ref[:, :16, :] = pack(*forward(key_value, *tables_in))
    spec_ref[:, 16:, :] = pack(*forward(square(taps_ref).astype(BF16), *tables_in))


def mix_for(weight_ref, pieces, shift, by_row):
    place = lax.axis_index("tensor")
    near, line = place // RING, place % RING
    target = near * RING + (line + shift) % RING
    totals = []
    for c in range(CH):
        total = None
        for half, piece in enumerate(pieces):
            source = (near ^ half) * RING + line
            for i in range(CH):
                to, of = target * CH + c, source * CH + i
                weight = weight_ref[to, of] if by_row else weight_ref[of, to]
                part = weight * piece[i * SIDE : (i + 1) * SIDE]
                total = part if total is None else total + part
        totals.append(total)
    return jnp.concatenate(totals, axis=0)


def mix_parts(weight_ref, pieces, mine_ref, other_refs, by_row):
    mine_ref[...] = mix_for(weight_ref, pieces, 0, by_row)
    for shift, ref in enumerate(other_refs, 1):
        ref[...] = mix_for(weight_ref, pieces, shift, by_row).astype(BF16)


def grad_mix_kernel(weight_ref, near_ref, far_ref, mine_ref, *other_refs):
    mix_parts(weight_ref, [square(near_ref), square(far_ref)], mine_ref, other_refs, True)


def out_mix_kernel(weight_ref, near_ref, far_ref, mine_ref, *other_refs):
    pieces = [near_ref[...].astype(F32), far_ref[...].astype(F32)]
    mix_parts(weight_ref, pieces, mine_ref, other_refs, False)


def total_of(mine_ref, other_refs):
    total = mine_ref[...]
    for ref in other_refs:
        total = total + ref[...].astype(F32)
    return total


def load(spec_ref, sig, buf_ref, slot):
    both = spec_ref[:, 16 * sig : 16 * sig + 16, :].astype(F32)
    buf_ref[slot, 0] = both[:, :PIECE]
    buf_ref[slot, 1] = both[:, PIECE:]


def alternate():
    row = lax.broadcasted_iota(jnp.int32, (PIECE, SIDE), 0)
    return jnp.where(row % 2 == 0, 1.0, -1.0).astype(F32)


def put(out_ref, blk, sig, real, imag):
    both = jnp.concatenate([real, imag], axis=0)
    out_ref[blk, 16 * sig : 16 * sig + 16, :] = both.astype(BF16)


def add(total, real, imag):
    return (real, imag) if total is None else (total[0] + real, total[1] + imag)


def convolve(buf_ref, out_ref, sign):
    def at(slot, blk):
        return buf_ref[slot, 0, blk], buf_ref[slot, 1, blk]

    last = None
    for base in range(0, BLOCKS, TILE):
        sums = [None] * TILE
        window = {}
        for j in range(base + TILE):
            hr, hi = at(1, j)
            for o in range(TILE):
                blk = base + o - j
                if blk < 0:
                    continue
                if blk not in window:
                    window[blk] = at(0, blk)
                xr, xi = window[blk]
                sums[o] = add(sums[o], hr * xr - hi * xi, hr * xi + hi * xr)
        for o in range(TILE):
            real, imag = sums[o]
            if last is not None:
                real, imag = real - sign * last[1], imag + sign * last[0]
            put(out_ref, base + o, 0, real, imag)
            last = sums[o]


def correlate(buf_ref, out_ref, sign, other, sig):
    def at(slot, blk):
        return buf_ref[slot, 0, blk], buf_ref[slot, 1, blk]

    after = None
    for base in range(BLOCKS - TILE, -1, -TILE):
        sums = [None] * TILE
        window = {}
        for j in range(BLOCKS - base):
            hr, hi = at(other, j)
            for o in range(TILE):
                blk = base + o + j
                if blk >= BLOCKS:
                    continue
                if blk not in window:
                    window[blk] = at(2, blk)
                gr, gi = window[blk]
                sums[o] = add(sums[o], gr * hr + gi * hi, gi * hr - gr * hi)
        for o in range(TILE - 1, -1, -1):
            real, imag = sums[o]
            if after is not None:
                real, imag = real + sign * after[1], imag - sign * after[0]
            put(out_ref, base + o, sig, real, imag)
            after = sums[o]


def convolve_kernel(spec_ref, grad_ref, out_ref, buf_ref):
    out_ref[:, 16:, :] = grad_ref[...]
    load(spec_ref, 0, buf_ref, 0)
    load(spec_ref, 1, buf_ref, 1)
    convolve(buf_ref, out_ref, alternate())


def grad_kernel(
    mine_ref, r1_ref, r2_ref, r3_ref, query_ref, first_ref, turn_ref, second_ref,
    gated_ref, inner_ref, out_ref,
):
    grad_gated = total_of(mine_ref, (r1_ref, r2_ref, r3_ref))
    gated_ref[...] = grad_gated
    grad_inner = (grad_gated * square(query_ref)).astype(BF16)
    inner_ref[...] = grad_inner
    out_ref[...] = pack(*forward(grad_inner, first_ref[...], turn_ref[...], second_ref[...]))


def correlate_kernel(spec_ref, rows_ref, out_ref, buf_ref):
    load(spec_ref, 0, buf_ref, 0)
    load(spec_ref, 1, buf_ref, 1)
    load(rows_ref, 1, buf_ref, 2)
    sign = alternate()
    correlate(buf_ref, out_ref, sign, 1, 0)
    correlate(buf_ref, out_ref, sign, 0, 1)


def gate_kernel(
    skip_ref, rows_ref, kv_ref, query_ref, gated_ref, first_ref, turn_ref, second_ref,
    out_ref, grad_query_ref,
):
    convolved = inverse(rows_ref[:, :16, :], first_ref[...], turn_ref[...], second_ref[...])
    inner_sum = convolved + skip_rows(skip_ref) * kv_ref[...].astype(F32)
    out_ref[...] = (square(query_ref) * inner_sum).astype(BF16)
    grad_query_ref[...] = (gated_ref[...] * inner_sum).reshape(CH, BLOCK).astype(BF16)


def skip_rows(skip_ref):
    row = lax.broadcasted_iota(jnp.int32, (ROWS, SIDE), 0)
    return jnp.where(row < SIDE, skip_ref[CH * GROUP, 0], skip_ref[CH * GROUP, 1])


def grads_kernel(
    skip_ref, rows_ref, inner_ref, key_ref, value_ref, first_ref, turn_ref, second_ref,
    grad_key_ref, grad_value_ref, grad_taps_ref, *, scale,
):
    tables_in = (first_ref[...], turn_ref[...], second_ref[...])
    source = inverse(rows_ref[:, :16, :], *tables_in)
    source = source + skip_rows(skip_ref) * inner_ref[...].astype(F32)
    source = source.reshape(CH, BLOCK)
    grad_key_ref[...] = (source * value_ref[...].astype(F32)).astype(BF16)
    grad_value_ref[...] = (source * key_ref[...].astype(F32)).astype(BF16)
    taps = inverse(rows_ref[:, 16:, :], *tables_in) * scale
    grad_taps_ref[...] = taps.reshape(CH, BLOCK)


def output_kernel(mine_ref, r1_ref, r2_ref, r3_ref, out_ref):
    both = total_of(mine_ref, (r1_ref, r2_ref, r3_ref))
    out_ref[...] = both.reshape(CH, BLOCK).astype(BF16)


def call(kernel, outs, operands, smem=0, scratch=(), place=VMEM, limit=48):
    return pl.pallas_call(
        kernel,
        out_shape=[jax.ShapeDtypeStruct(shape, dtype) for shape, dtype in outs],
        in_specs=[SMEM] * smem + [place] * (len(operands) - smem),
        out_specs=[VMEM] * len(outs),
        scratch_shapes=list(scratch),
        compiler_params=pltpu.CompilerParams(vmem_limit_bytes=limit * 1024 * 1024),
    )(*operands)


def exchange(blocks):
    return lax.all_to_all(blocks, "seq", split_axis=0, concat_axis=0, tiled=True)


def along_y(arrays):
    received = []
    for shift, array in enumerate(arrays, 1):
        pairs = [
            (near * RING + line, near * RING + (line + shift) % RING)
            for near in range(GROUP // RING)
            for line in range(RING)
        ]
        received.append(lax.ppermute(array, "tensor", pairs))
    return received


def across(array):
    return lax.ppermute(array, "tensor", [(i, (i + RING) % GROUP) for i in range(GROUP)])


def body(queries, key_feats, value_feats, filter_taps, skip_gain, out_weight, out_grad):
    first, first_t, turn, second, second_t = tables()
    forward_tables = (first, turn, second)
    inverse_tables = (first_t, turn, second_t)
    skip_row = jnp.concatenate([skip_gain, jnp.zeros(2 * CH * GROUP - CH - CH * GROUP, F32)])
    weight = jnp.concatenate([out_weight.astype(F32), skip_row[None]], axis=0)
    square_shape = (ROWS, SIDE)
    tokens = (CH, BLOCK)
    one, two = (BLOCKS, 16, SIDE), (BLOCKS, 32, SIDE)
    parts = [(square_shape, F32)] + [(square_shape, BF16)] * (RING - 1)

    key_value, spec = call(
        source_kernel,
        [(square_shape, BF16), (two, BF16)],
        (key_feats, value_feats, filter_taps, *forward_tables),
        scratch=[
            *[pltpu.VMEM(tokens, BF16)] * 3,
            *[pltpu.VMEM(table.shape, table.dtype) for table in forward_tables],
            pltpu.SemaphoreType.DMA((6,)),
        ],
        place=HBM,
        limit=62,
    )
    spec, far = lax.optimization_barrier((spec, across(out_grad)))
    spec = exchange(spec)
    mine, *others = call(grad_mix_kernel, parts, (weight, out_grad, far), smem=1)
    others = along_y(others)
    grad_gated, grad_inner, grad_spec = call(
        grad_kernel,
        [(square_shape, F32), (square_shape, BF16), (one, BF16)],
        (mine, *others, queries, *forward_tables),
    )
    (rows,) = call(
        convolve_kernel,
        [(two, BF16)],
        (spec, grad_spec),
        scratch=[pltpu.VMEM((2, 2, BLOCKS, PIECE, SIDE), F32)],
    )
    rows = exchange(rows)
    gated, grad_queries = call(
        gate_kernel,
        [(square_shape, BF16), (tokens, BF16)],
        (weight, rows, key_value, queries, grad_gated, *inverse_tables),
        smem=1,
    )
    (corr,) = call(
        correlate_kernel,
        [(two, BF16)],
        (spec, rows),
        scratch=[pltpu.VMEM((3, 2, BLOCKS, PIECE, SIDE), F32)],
    )
    corr, far = lax.optimization_barrier((corr, across(gated)))
    corr = exchange(corr)
    mine, *others = call(out_mix_kernel, parts, (weight, gated, far), smem=1)
    others = along_y(others)

    def grads(*refs):
        grads_kernel(*refs, scale=(BLOCKS * BLOCK) ** -0.5)

    grad_keys, grad_values, grad_taps = call(
        grads,
        [(tokens, BF16), (tokens, BF16), (tokens, F32)],
        (weight, corr, grad_inner, key_feats, value_feats, *inverse_tables),
        smem=1,
    )
    (output,) = call(output_kernel, [(tokens, BF16)], (mine, *others))
    return (output, grad_queries, grad_keys, grad_values, grad_taps)


def solution(mesh):
    assert dict(mesh.shape) == {"tensor": GROUP, "seq": BLOCKS}
    placed = P("tensor", "seq")
    return jax.shard_map(
        body,
        mesh=mesh,
        in_specs=(placed, placed, placed, placed, P("tensor"), P(), placed),
        out_specs=(placed,) * 5,
        check_vma=False,
    )
```

```python
import math

import jax
import jax.numpy as jnp
import numpy as np
from jax import lax
from jax.experimental import pallas as pl
from jax.experimental.pallas import tpu as pltpu
from jax.sharding import PartitionSpec as P

F32 = jnp.float32
BF16 = jnp.bfloat16
CH = 2
GROUP = 8
RING = 4
CHUNK = 16
WEIGHTS = RING * CH * 2 * CH
TILE = 4
BLOCKS = 32
SIDE = 128
ROWS = CH * SIDE
BLOCK = SIDE * SIDE
LENGTH = 2 * BLOCK
PIECE = ROWS // BLOCKS
VMEM = pl.BlockSpec(memory_space=pltpu.VMEM)
COST = pl.CostEstimate(flops=10000000000, bytes_accessed=1000000, transcendentals=0)
SMEM = pl.BlockSpec(memory_space=pltpu.SMEM)
HBM = pl.BlockSpec(memory_space=pltpu.HBM)
ANY = pl.BlockSpec(memory_space=pl.ANY)


def tables():
    side = np.arange(SIDE)
    angle = 2 * np.pi * (side[:, None] + 0.5) * side[None, :] / (2 * SIDE)
    first = np.concatenate([np.cos(angle), -np.sin(angle)], axis=0)
    angle = 2 * np.pi * (side[:, None] + 0.5) * side[None, :] / LENGTH
    turn = np.stack([np.cos(angle), np.sin(angle)])
    angle = 2 * np.pi * side[:, None] * side[None, :] / SIDE
    second = np.stack([np.cos(angle), np.sin(angle)])
    return (
        jnp.asarray(first, BF16),
        jnp.asarray(first.T, BF16),
        jnp.asarray(turn, F32),
        jnp.asarray(second, BF16),
    )


def square(ref):
    return ref[...].astype(F32).reshape(ROWS, SIDE)


def second_stage(second, sign):
    cos, sin = second[0], second[1]
    top = [cos, sin] if sign > 0 else [cos, -sin]
    low = [-sin, cos] if sign > 0 else [sin, cos]
    return jnp.concatenate(
        [jnp.concatenate(top, axis=1), jnp.concatenate(low, axis=1)], axis=0
    )


def forward(signal, first, turn, second):
    both = jnp.concatenate([signal[:SIDE], signal[SIDE:]], axis=1)
    stage = jnp.dot(first, both, preferred_element_type=F32)
    cos, sin = turn[0], turn[1]
    turned = []
    for c in range(CH):
        real, imag = (stage[p * SIDE : (p + 1) * SIDE, c * SIDE : (c + 1) * SIDE] for p in (0, 1))
        turned.append(
            jnp.concatenate(
                [(real * cos + imag * sin).astype(BF16), (imag * cos - real * sin).astype(BF16)],
                axis=1,
            )
        )
    spec = jnp.dot(
        jnp.concatenate(turned, axis=0), second_stage(second, -1), preferred_element_type=F32
    )
    parts = [spec[:, p * SIDE : (p + 1) * SIDE].reshape(BLOCKS, PIECE, SIDE) for p in (0, 1)]
    return jnp.concatenate(parts, axis=1).astype(BF16)


def inverse(rows, first_t, turn, second):
    rows = rows.astype(F32)
    real = rows[:, :PIECE].reshape(ROWS, SIDE)
    imag = rows[:, PIECE:].reshape(ROWS, SIDE)
    spec = jnp.concatenate([real.astype(BF16), imag.astype(BF16)], axis=1)
    stage = jnp.dot(spec, second_stage(second, 1), preferred_element_type=F32)
    cos, sin = turn[0], turn[1]
    turned = []
    for c in range(CH):
        real, imag = (stage[c * SIDE : (c + 1) * SIDE, p * SIDE : (p + 1) * SIDE] for p in (0, 1))
        turned.append(
            jnp.concatenate(
                [(real * cos - imag * sin).astype(BF16), (imag * cos + real * sin).astype(BF16)],
                axis=0,
            )
        )
    both = jnp.dot(first_t, jnp.concatenate(turned, axis=1), preferred_element_type=F32)
    both = both * (2.0 / LENGTH)
    return jnp.concatenate([both[:, :SIDE], both[:, SIDE:]], axis=0)


def source_kernel(
    key_hbm, value_hbm, taps_hbm, weight_hbm, skip_hbm, first_hbm, turn_hbm, second_hbm,
    table_ref, kv_hbm, spec_hbm,
    key_ref, value_ref, taps_ref, weight_ref, skip_ref, first_ref, turn_ref, second_ref,
    kv_ref, spec_ref, sems,
):
    copies = []

    def send(src, dst):
        copy = pltpu.make_async_copy(src, dst, sems.at[len(copies)])
        copy.start()
        copies.append(copy)

    def part(sig):
        return spec_hbm.at[:, pl.ds(16 * sig, 16), :]

    send(taps_hbm, taps_ref)
    send(first_hbm, first_ref)
    send(turn_hbm, turn_ref)
    send(second_hbm, second_ref)
    send(key_hbm, key_ref)
    send(value_hbm, value_ref)
    send(weight_hbm, weight_ref)
    send(skip_hbm, skip_ref)
    for copy in copies:
        copy.wait()
    arrived = len(copies)
    tables_in = (first_ref[...], turn_ref[...], second_ref[...])
    spec_ref[1] = forward(square(taps_ref).astype(BF16), *tables_in)
    send(spec_ref.at[1], part(1))
    key_value = (square(key_ref) * square(value_ref)).astype(BF16)
    kv_ref[...] = key_value
    send(kv_ref, kv_hbm)
    spec_ref[0] = forward(key_value, *tables_in)
    send(spec_ref.at[0], part(0))
    table_ref[:WEIGHTS, :] = weight_rows(weight_ref[...], True)
    table_ref[WEIGHTS : 2 * WEIGHTS, :] = weight_rows(weight_ref[...], False)
    row = lax.broadcasted_iota(jnp.int32, (8, SIDE), 0)
    table_ref[2 * WEIGHTS :, :] = jnp.where(row == 0, skip_ref[0], skip_ref[1])
    for copy in copies[arrived:]:
        copy.wait()


def weight_rows(weight, by_row):
    place = lax.axis_index("tensor")
    near, line = place // RING, place % RING
    shape = (WEIGHTS, CH * GROUP)
    row = lax.broadcasted_iota(jnp.int32, shape, 0)
    column = lax.broadcasted_iota(jnp.int32, shape, 1)
    shift, chan, half, i = row // 8, row // 4 % 2, row // 2 % 2, row % 2
    to = (near * RING + (line + shift) % RING) * CH + chan
    of = ((near ^ half) * RING + line) * CH + i
    first, last = (to, of) if by_row else (of, to)
    pick = jnp.where(column == first, 1.0, 0.0).astype(BF16)
    picked = jnp.dot(pick, weight, preferred_element_type=F32)
    value = jnp.sum(jnp.where(column == last, picked, 0.0), axis=1, keepdims=True)
    return jnp.broadcast_to(value, (WEIGHTS, SIDE))


def mix_parts(table_ref, first_row, pieces, mine_ref, other_refs):
    for base in range(0, SIDE, CHUNK):
        loaded = [
            piece[i * SIDE + base : i * SIDE + base + CHUNK, :].astype(F32)
            for piece in pieces
            for i in range(CH)
        ]
        for shift in range(RING):
            for c in range(CH):
                total = None
                for i, value in enumerate(loaded):
                    row = first_row + (shift * CH + c) * 4 + i
                    part = table_ref[row : row + 1, :] * value
                    total = part if total is None else total + part
                place_rows = pl.ds(c * SIDE + base, CHUNK)
                if shift == 0:
                    mine_ref[place_rows, :] = total
                else:
                    other_refs[shift - 1][place_rows, :] = total.astype(BF16)


def grad_mix_kernel(table_ref, near_ref, far_ref, mine_ref, *rest):
    other_refs, squares = rest[: RING - 1], rest[RING - 1 :]
    for ref, buf in zip((near_ref, far_ref), squares):
        buf[...] = square(ref)
    mix_parts(table_ref, 0, squares, mine_ref, other_refs)


def out_mix_kernel(table_ref, near_ref, far_ref, mine_ref, *other_refs):
    mix_parts(table_ref, WEIGHTS, (near_ref, far_ref), mine_ref, other_refs)


def total_of(mine_ref, other_refs):
    total = mine_ref[...]
    for ref in other_refs:
        total = total + ref[...].astype(F32)
    return total


def load(spec_ref, sig, buf_ref, slot):
    both = spec_ref[:, 16 * sig : 16 * sig + 16, :].astype(F32)
    buf_ref[slot, 0] = both[:, :PIECE]
    buf_ref[slot, 1] = both[:, PIECE:]


def alternate():
    row = lax.broadcasted_iota(jnp.int32, (PIECE, SIDE), 0)
    return jnp.where(row % 2 == 0, 1.0, -1.0).astype(F32)


def put(out_ref, blk, sig, real, imag):
    both = jnp.concatenate([real, imag], axis=0)
    out_ref[blk, 16 * sig : 16 * sig + 16, :] = both.astype(BF16)


def add(total, parts):
    return parts if total is None else tuple(t + p for t, p in zip(total, parts))


def convolve(buf_ref, out_ref, sign):
    def at(slot, blk):
        return buf_ref[slot, 0, blk], buf_ref[slot, 1, blk]

    last = None
    for base in range(0, BLOCKS, TILE):
        sums = [None] * TILE
        window = {}
        for j in range(base + TILE):
            hr, hi = at(1, j)
            plus, minus = hr + hi, hi - hr
            for o in range(TILE):
                blk = base + o - j
                if blk < 0:
                    continue
                if blk not in window:
                    xr, xi = at(0, blk)
                    window[blk] = (xr, xi, xr + xi)
                xr, xi, both = window[blk]
                sums[o] = add(sums[o], (hr * both, xi * plus, xr * minus))
        for o in range(TILE):
            common, of_real, of_imag = sums[o]
            total = (common - of_real, common + of_imag)
            real, imag = total
            if last is not None:
                real, imag = real - sign * last[1], imag + sign * last[0]
            put(out_ref, base + o, 0, real, imag)
            last = total


def correlate(buf_ref, out_ref, sign, other, sig):
    def at(slot, blk):
        return buf_ref[slot, 0, blk], buf_ref[slot, 1, blk]

    after = None
    for base in range(BLOCKS - TILE, -1, -TILE):
        sums = [None] * TILE
        window = {}
        for j in range(BLOCKS - base):
            hr, hi = at(other, j)
            plus, minus = hr + hi, hr - hi
            for o in range(TILE):
                blk = base + o + j
                if blk >= BLOCKS:
                    continue
                if blk not in window:
                    gr, gi = at(2, blk)
                    window[blk] = (gr, gi, gr + gi)
                gr, gi, both = window[blk]
                sums[o] = add(sums[o], (hr * both, gi * minus, gr * plus))
        for o in range(TILE - 1, -1, -1):
            common, of_real, of_imag = sums[o]
            total = (common - of_real, common - of_imag)
            real, imag = total
            if after is not None:
                real, imag = real + sign * after[1], imag - sign * after[0]
            put(out_ref, base + o, sig, real, imag)
            after = total


def convolve_kernel(spec_ref, grad_ref, out_ref, buf_ref):
    out_ref[:, 16:, :] = grad_ref[...]
    load(spec_ref, 0, buf_ref, 0)
    load(spec_ref, 1, buf_ref, 1)
    convolve(buf_ref, out_ref, alternate())


def grad_kernel(
    mine_ref, r1_ref, r2_ref, r3_ref, query_ref, first_ref, turn_ref, second_ref,
    gated_ref, inner_ref, out_ref,
):
    grad_gated = total_of(mine_ref, (r1_ref, r2_ref, r3_ref))
    gated_ref[...] = grad_gated
    grad_inner = (grad_gated * square(query_ref)).astype(BF16)
    inner_ref[...] = grad_inner
    out_ref[...] = forward(grad_inner, first_ref[...], turn_ref[...], second_ref[...])


def correlate_kernel(
    spec_ref, rows_ref, inner_sum_ref, gated_ref, out_hbm, grad_query_hbm,
    buf_ref, out_ref, grad_query_ref, sems,
):
    grad_query_ref[...] = (gated_ref[...] * inner_sum_ref[...]).reshape(CH, BLOCK).astype(BF16)
    query_copy = pltpu.make_async_copy(grad_query_ref, grad_query_hbm, sems.at[0])
    query_copy.start()
    load(spec_ref, 0, buf_ref, 0)
    load(spec_ref, 1, buf_ref, 1)
    load(rows_ref, 1, buf_ref, 2)
    sign = alternate()
    copies = []
    for sig, other in ((0, 1), (1, 0)):
        correlate(buf_ref, out_ref.at[sig], sign, other, 0)
        copy = pltpu.make_async_copy(
            out_ref.at[sig], out_hbm.at[:, pl.ds(16 * sig, 16), :], sems.at[1 + sig]
        )
        copy.start()
        copies.append(copy)
    for copy in copies:
        copy.wait()
    query_copy.wait()


def gate_kernel(
    skip_ref, rows_ref, kv_ref, query_ref, first_ref, turn_ref, second_ref, out_ref, inner_sum_ref
):
    convolved = inverse(rows_ref[:, :16, :], first_ref[...], turn_ref[...], second_ref[...])
    inner_sum = convolved + skip_rows(skip_ref) * kv_ref[...].astype(F32)
    inner_sum_ref[...] = inner_sum
    out_ref[...] = (square(query_ref) * inner_sum).astype(BF16)


def skip_rows(table_ref):
    return jnp.concatenate(
        [
            jnp.broadcast_to(table_ref[2 * WEIGHTS + c : 2 * WEIGHTS + c + 1, :], (SIDE, SIDE))
            for c in range(CH)
        ],
        axis=0,
    )


def last_kernel(
    table_ref, rows_ref, inner_ref, key_ref, value_ref, first_ref, turn_ref, second_ref,
    mine_ref, r1_ref, r2_ref, r3_ref,
    out_hbm, grad_key_hbm, grad_value_hbm, grad_taps_hbm,
    out_ref, grad_key_ref, grad_value_ref, grad_taps_ref, sems, *, scale,
):
    copies = []

    def send(src, dst):
        copy = pltpu.make_async_copy(src, dst, sems.at[len(copies)])
        copy.start()
        copies.append(copy)

    both = total_of(mine_ref, (r1_ref, r2_ref, r3_ref))
    out_ref[...] = both.reshape(CH, BLOCK).astype(BF16)
    send(out_ref, out_hbm)
    tables_in = (first_ref[...], turn_ref[...], second_ref[...])
    taps = inverse(rows_ref[:, 16:, :], *tables_in) * scale
    grad_taps_ref[...] = taps.reshape(CH, BLOCK)
    send(grad_taps_ref, grad_taps_hbm)
    source = inverse(rows_ref[:, :16, :], *tables_in)
    source = source + skip_rows(table_ref) * inner_ref[...].astype(F32)
    source = source.reshape(CH, BLOCK)
    grad_key_ref[...] = (source * value_ref[...].astype(F32)).astype(BF16)
    send(grad_key_ref, grad_key_hbm)
    grad_value_ref[...] = (source * key_ref[...].astype(F32)).astype(BF16)
    send(grad_value_ref, grad_value_hbm)
    for copy in copies:
        copy.wait()


def call(kernel, outs, operands, smem=0, scratch=(), place=VMEM, limit=48, cost=None, out_place=VMEM):
    return pl.pallas_call(
        kernel,
        out_shape=[jax.ShapeDtypeStruct(shape, dtype) for shape, dtype in outs],
        in_specs=[SMEM] * smem + [place] * (len(operands) - smem),
        out_specs=out_place if isinstance(out_place, list) else [out_place] * len(outs),
        scratch_shapes=list(scratch),
        cost_estimate=cost,
        compiler_params=pltpu.CompilerParams(vmem_limit_bytes=limit * 1024 * 1024),
    )(*operands)


def exchange(blocks):
    return lax.all_to_all(blocks, "seq", split_axis=0, concat_axis=0, tiled=True)


def along_y(arrays):
    received = []
    for shift, array in enumerate(arrays, 1):
        pairs = [
            (near * RING + line, near * RING + (line + shift) % RING)
            for near in range(GROUP // RING)
            for line in range(RING)
        ]
        received.append(lax.ppermute(array, "tensor", pairs))
    return received


def across(array):
    return lax.ppermute(array, "tensor", [(i, (i + RING) % GROUP) for i in range(GROUP)])


def body(queries, key_feats, value_feats, filter_taps, skip_gain, out_weight, out_grad):
    first, first_t, turn, second = tables()
    forward_tables = (first, turn, second)
    inverse_tables = (first_t, turn, second)
    square_shape = (ROWS, SIDE)
    tokens = (CH, BLOCK)
    one, two = (BLOCKS, 16, SIDE), (BLOCKS, 32, SIDE)
    parts = [(square_shape, F32)] + [(square_shape, BF16)] * (RING - 1)

    first_inputs = (key_feats, value_feats, filter_taps, out_weight, skip_gain, *forward_tables)
    table, key_value, spec = call(
        source_kernel,
        [((2 * WEIGHTS + 8, SIDE), F32), (square_shape, BF16), (two, BF16)],
        [pltpu.with_memory_space_constraint(array, pltpu.HBM) for array in first_inputs],
        scratch=[
            *[pltpu.VMEM(tokens, BF16)] * 3,
            pltpu.VMEM(out_weight.shape, BF16),
            pltpu.SMEM((CH,), F32),
            *[pltpu.VMEM(array.shape, array.dtype) for array in forward_tables],
            pltpu.VMEM(square_shape, BF16),
            pltpu.VMEM((2, *one), BF16),
            pltpu.SemaphoreType.DMA((11,)),
        ],
        place=HBM,
        limit=32,
        out_place=[VMEM, ANY, ANY],
    )
    far = across(out_grad)
    spec = exchange(spec)
    mine, *others = call(
        grad_mix_kernel,
        parts,
        (table, out_grad, far),
        scratch=[pltpu.VMEM(square_shape, F32)] * 2,
        cost=COST,
    )
    others = along_y(others)
    grad_gated, grad_inner, grad_spec = call(
        grad_kernel,
        [(square_shape, F32), (square_shape, BF16), (one, BF16)],
        (mine, *others, queries, *forward_tables),
    )
    (rows,) = call(
        convolve_kernel,
        [(two, BF16)],
        (spec, grad_spec),
        scratch=[pltpu.VMEM((2, 2, BLOCKS, PIECE, SIDE), F32)],
    )
    rows = exchange(rows)
    gated, inner_sum = call(
        gate_kernel,
        [(square_shape, BF16), (square_shape, F32)],
        (table, rows, key_value, queries, *inverse_tables),
    )
    far = across(gated)
    rows, gated = lax.optimization_barrier((rows, gated))
    corr, grad_queries = call(
        correlate_kernel,
        [(two, BF16), (tokens, BF16)],
        (spec, rows, inner_sum, grad_gated),
        scratch=[
            pltpu.VMEM((3, 2, BLOCKS, PIECE, SIDE), F32),
            pltpu.VMEM((2, *one), BF16),
            pltpu.VMEM(tokens, BF16),
            pltpu.SemaphoreType.DMA((3,)),
        ],
        out_place=ANY,
    )
    corr = exchange(corr)
    mine, *others = call(out_mix_kernel, parts, (table, gated, far), cost=COST)
    others = along_y(others)

    def last(*refs):
        last_kernel(*refs, scale=(BLOCKS * BLOCK) ** -0.5)

    output, grad_keys, grad_values, grad_taps = call(
        last,
        [(tokens, BF16), (tokens, BF16), (tokens, BF16), (tokens, F32)],
        (table, corr, grad_inner, key_feats, value_feats, *inverse_tables, mine, *others),
        scratch=[
            *[pltpu.VMEM(tokens, BF16)] * 3,
            pltpu.VMEM(tokens, F32),
            pltpu.SemaphoreType.DMA((4,)),
        ],
        out_place=ANY,
    )
    return (output, grad_queries, grad_keys, grad_values, grad_taps)


def solution(mesh):
    assert dict(mesh.shape) == {"tensor": GROUP, "seq": BLOCKS}
    placed = P("tensor", "seq")
    return jax.shard_map(
        body,
        mesh=mesh,
        in_specs=(placed, placed, placed, placed, P("tensor"), P(), placed),
        out_specs=(placed,) * 5,
        check_vma=False,
    )
```

```python
import functools

import jax
import jax.numpy as jnp
import numpy as np
from jax import lax
from jax.experimental import pallas as pl
from jax.experimental.pallas import tpu as pltpu
from jax.sharding import PartitionSpec as P

F32 = jnp.float32
BF16 = jnp.bfloat16
CH = 2
GROUP = 8
RING = 4
CHUNK = 16
WEIGHTS = RING * CH * 2 * CH
TILE = 4
BLOCKS = 32
SIDE = 128
ROWS = CH * SIDE
BLOCK = SIDE * SIDE
LENGTH = 2 * BLOCK
PIECE = ROWS // BLOCKS
VMEM = pl.BlockSpec(memory_space=pltpu.VMEM)
COST = pl.CostEstimate(flops=10000000000, bytes_accessed=1000000, transcendentals=0)
HBM = pl.BlockSpec(memory_space=pltpu.HBM)
ANY = pl.BlockSpec(memory_space=pl.ANY)


def tables():
    side = np.arange(SIDE)
    angle = 2 * np.pi * (side[:, None] + 0.5) * side[None, :] / (2 * SIDE)
    first = np.concatenate([np.cos(angle), -np.sin(angle)], axis=0)
    angle = 2 * np.pi * (side[:, None] + 0.5) * side[None, :] / LENGTH
    turn = np.stack([np.cos(angle), np.sin(angle)])
    angle = 2 * np.pi * side[:, None] * side[None, :] / SIDE
    second = np.stack([np.cos(angle), np.sin(angle)])
    return (
        jnp.asarray(first, BF16),
        jnp.asarray(first.T, BF16),
        jnp.asarray(turn, F32),
        jnp.asarray(second, BF16),
    )


def square(ref):
    return ref[...].astype(F32).reshape(ROWS, SIDE)


def second_stage(second, sign):
    cos, sin = second[0], second[1]
    top = [cos, sin] if sign > 0 else [cos, -sin]
    low = [-sin, cos] if sign > 0 else [sin, cos]
    return jnp.concatenate(
        [jnp.concatenate(top, axis=1), jnp.concatenate(low, axis=1)], axis=0
    )


def forward(signals, first, turn, second):
    both = [jnp.concatenate([signal[:SIDE], signal[SIDE:]], axis=1) for signal in signals]
    stages = jnp.dot(first, jnp.concatenate(both, axis=1), preferred_element_type=F32)
    cos, sin = turn[0], turn[1]
    turned = []
    for c in range(CH * len(signals)):
        real, imag = (
            stages[p * SIDE : (p + 1) * SIDE, c * SIDE : (c + 1) * SIDE] for p in (0, 1)
        )
        turned.append(
            jnp.concatenate(
                [(real * cos + imag * sin).astype(BF16), (imag * cos - real * sin).astype(BF16)],
                axis=1,
            )
        )
    spec = jnp.dot(
        jnp.concatenate(turned, axis=0), second_stage(second, -1), preferred_element_type=F32
    )
    results = []
    for i in range(len(signals)):
        rows = spec[i * ROWS : (i + 1) * ROWS]
        parts = [rows[:, p * SIDE : (p + 1) * SIDE].reshape(BLOCKS, PIECE, SIDE) for p in (0, 1)]
        results.append(jnp.concatenate(parts, axis=1).astype(BF16))
    return results


def inverse(pieces, first_t, turn, second):
    specs = []
    for rows in pieces:
        rows = rows.astype(F32)
        real = rows[:, :PIECE].reshape(ROWS, SIDE)
        imag = rows[:, PIECE:].reshape(ROWS, SIDE)
        specs.append(jnp.concatenate([real.astype(BF16), imag.astype(BF16)], axis=1))
    stages = jnp.dot(
        jnp.concatenate(specs, axis=0), second_stage(second, 1), preferred_element_type=F32
    )
    cos, sin = turn[0], turn[1]
    turned = []
    for c in range(CH * len(pieces)):
        real, imag = (
            stages[c * SIDE : (c + 1) * SIDE, p * SIDE : (p + 1) * SIDE] for p in (0, 1)
        )
        turned.append(
            jnp.concatenate(
                [(real * cos - imag * sin).astype(BF16), (imag * cos + real * sin).astype(BF16)],
                axis=0,
            )
        )
    both = jnp.dot(first_t, jnp.concatenate(turned, axis=1), preferred_element_type=F32)
    both = both * (2.0 / LENGTH)
    columns = [both[:, c * SIDE : (c + 1) * SIDE] for c in range(CH * len(pieces))]
    return [
        jnp.concatenate(columns[CH * i : CH * i + CH], axis=0) for i in range(len(pieces))
    ]


def source_kernel(
    key_hbm, value_hbm, taps_hbm, weight_hbm, skip_hbm, first_hbm, turn_hbm, second_hbm,
    table_ref, kv_ref, spec_hbm,
    key_ref, value_ref, taps_ref, weight_ref, skip_ref, first_ref, turn_ref, second_ref,
    spec_ref, sems,
):
    copies = []

    def send(src, dst):
        copy = pltpu.make_async_copy(src, dst, sems.at[len(copies)])
        copy.start()
        copies.append(copy)

    send(key_hbm, key_ref)
    send(value_hbm, value_ref)
    send(taps_hbm, taps_ref)
    send(first_hbm, first_ref)
    send(turn_hbm, turn_ref)
    send(second_hbm, second_ref)
    send(weight_hbm, weight_ref)
    send(skip_hbm, skip_ref)
    for copy in copies:
        copy.wait()
    arrived = len(copies)
    key_value = (square(key_ref) * square(value_ref)).astype(BF16)
    kv_ref[...] = key_value
    spec_ref[0], spec_ref[1] = forward(
        [key_value, square(taps_ref).astype(BF16)],
        first_ref[...],
        turn_ref[...],
        second_ref[...],
    )
    for sig in range(2):
        send(spec_ref.at[sig], spec_hbm.at[:, pl.ds(16 * sig, 16), :])
    table_ref[:WEIGHTS, :] = weight_rows(weight_ref[...], True)
    table_ref[WEIGHTS : 2 * WEIGHTS, :] = weight_rows(weight_ref[...], False)
    row = lax.broadcasted_iota(jnp.int32, (8, SIDE), 0)
    table_ref[2 * WEIGHTS :, :] = jnp.where(row == 0, skip_ref[0], skip_ref[1])
    for copy in copies[arrived:]:
        copy.wait()


def weight_rows(weight, by_row):
    place = lax.axis_index("tensor")
    near, line = place // RING, place % RING
    shape = (WEIGHTS, CH * GROUP)
    row = lax.broadcasted_iota(jnp.int32, shape, 0)
    column = lax.broadcasted_iota(jnp.int32, shape, 1)
    shift, chan, half, i = row // 8, row // 4 % 2, row // 2 % 2, row % 2
    to = (near * RING + (line + shift) % RING) * CH + chan
    of = ((near ^ half) * RING + line) * CH + i
    first, last = (to, of) if by_row else (of, to)
    pick = jnp.where(column == first, 1.0, 0.0).astype(BF16)
    picked = jnp.dot(pick, weight, preferred_element_type=F32)
    value = jnp.sum(jnp.where(column == last, picked, 0.0), axis=1, keepdims=True)
    return jnp.broadcast_to(value, (WEIGHTS, SIDE))


def mix_parts(table_ref, first_row, pieces, mine_ref, other_refs):
    for base in range(0, SIDE, CHUNK):
        loaded = [
            piece[i * SIDE + base : i * SIDE + base + CHUNK, :].astype(F32)
            for piece in pieces
            for i in range(CH)
        ]
        for shift in range(RING):
            for c in range(CH):
                total = None
                for i, value in enumerate(loaded):
                    row = first_row + (shift * CH + c) * 4 + i
                    part = table_ref[row : row + 1, :] * value
                    total = part if total is None else total + part
                place_rows = pl.ds(c * SIDE + base, CHUNK)
                if shift == 0:
                    mine_ref[place_rows, :] = total
                else:
                    other_refs[shift - 1][place_rows, :] = total.astype(BF16)


def grad_mix_kernel(table_ref, near_ref, far_ref, mine_ref, *rest):
    other_refs, squares = rest[: RING - 1], rest[RING - 1 :]
    for ref, buf in zip((near_ref, far_ref), squares):
        buf[...] = square(ref)
    mix_parts(table_ref, 0, squares, mine_ref, other_refs)


def out_mix_kernel(table_ref, near_ref, far_ref, mine_ref, *other_refs):
    mix_parts(table_ref, WEIGHTS, (near_ref, far_ref), mine_ref, other_refs)


def total_of(mine_ref, other_refs):
    total = mine_ref[...]
    for ref in other_refs:
        total = total + ref[...].astype(F32)
    return total


def load(spec_ref, sig, buf_ref, slot):
    both = spec_ref[:, 16 * sig : 16 * sig + 16, :].astype(F32)
    buf_ref[slot, 0] = both[:, :PIECE]
    buf_ref[slot, 1] = both[:, PIECE:]


def alternate():
    row = lax.broadcasted_iota(jnp.int32, (PIECE, SIDE), 0)
    return jnp.where(row % 2 == 0, 1.0, -1.0).astype(F32)


def put(out_ref, blk, sig, real, imag):
    both = jnp.concatenate([real, imag], axis=0)
    out_ref[blk, 16 * sig : 16 * sig + 16, :] = both.astype(BF16)


def add(total, parts):
    return parts if total is None else tuple(t + p for t, p in zip(total, parts))


def convolve(buf_ref, out_ref, sign):
    def at(slot, blk):
        return buf_ref[slot, 0, blk], buf_ref[slot, 1, blk]

    last = None
    for base in range(0, BLOCKS, TILE):
        sums = [None] * TILE
        window = {}
        for j in range(base + TILE):
            hr, hi = at(1, j)
            plus, minus = hr + hi, hi - hr
            for o in range(TILE):
                blk = base + o - j
                if blk < 0:
                    continue
                if blk not in window:
                    xr, xi = at(0, blk)
                    window[blk] = (xr, xi, xr + xi)
                xr, xi, both = window[blk]
                sums[o] = add(sums[o], (hr * both, xi * plus, xr * minus))
        for o in range(TILE):
            common, of_real, of_imag = sums[o]
            total = (common - of_real, common + of_imag)
            real, imag = total
            if last is not None:
                real, imag = real - sign * last[1], imag + sign * last[0]
            put(out_ref, base + o, 0, real, imag)
            last = total


def correlate(buf_ref, out_ref, sign, other, sig):
    def at(slot, blk):
        return buf_ref[slot, 0, blk], buf_ref[slot, 1, blk]

    after = None
    for base in range(BLOCKS - TILE, -1, -TILE):
        sums = [None] * TILE
        window = {}
        for j in range(BLOCKS - base):
            hr, hi = at(other, j)
            plus, minus = hr + hi, hr - hi
            for o in range(TILE):
                blk = base + o + j
                if blk >= BLOCKS:
                    continue
                if blk not in window:
                    gr, gi = at(2, blk)
                    window[blk] = (gr, gi, gr + gi)
                gr, gi, both = window[blk]
                sums[o] = add(sums[o], (hr * both, gi * minus, gr * plus))
        for o in range(TILE - 1, -1, -1):
            common, of_real, of_imag = sums[o]
            total = (common - of_real, common - of_imag)
            real, imag = total
            if after is not None:
                real, imag = real + sign * after[1], imag - sign * after[0]
            put(out_ref, base + o, sig, real, imag)
            after = total


def convolve_kernel(spec_ref, grad_ref, out_ref, buf_ref):
    out_ref[:, 16:, :] = grad_ref[...]
    load(spec_ref, 0, buf_ref, 0)
    load(spec_ref, 1, buf_ref, 1)
    convolve(buf_ref, out_ref, alternate())


def grad_kernel(
    mine_ref, r1_ref, r2_ref, r3_ref, query_ref, first_ref, turn_ref, second_ref,
    gated_ref, inner_ref, out_ref,
):
    grad_gated = total_of(mine_ref, (r1_ref, r2_ref, r3_ref))
    gated_ref[...] = grad_gated
    grad_inner = (grad_gated * square(query_ref)).astype(BF16)
    inner_ref[...] = grad_inner
    (out_ref[...],) = forward([grad_inner], first_ref[...], turn_ref[...], second_ref[...])


def correlate_kernel(half, spec_ref, rows_ref, inner_sum_ref, gated_ref, *refs):
    out_hbm, grad_query_hbm, buf_ref, out_ref, grad_query_ref, sems = refs[2 * half :]

    @pl.when(lax.axis_index("tensor") // RING == half)
    def _():
        grad_query_ref[...] = (
            (gated_ref[...] * inner_sum_ref[...]).reshape(CH, BLOCK).astype(BF16)
        )
        query_copy = pltpu.make_async_copy(grad_query_ref, grad_query_hbm, sems.at[0])
        query_copy.start()
        load(spec_ref, 0, buf_ref, 0)
        load(spec_ref, 1, buf_ref, 1)
        load(rows_ref, 1, buf_ref, 2)
        sign = alternate()
        copies = []
        for sig, other in ((0, 1), (1, 0)):
            correlate(buf_ref, out_ref.at[sig], sign, other, 0)
            copy = pltpu.make_async_copy(
                out_ref.at[sig], out_hbm.at[:, pl.ds(16 * sig, 16), :], sems.at[1 + sig]
            )
            copy.start()
            copies.append(copy)
        for copy in copies:
            copy.wait()
        query_copy.wait()


def gate_kernel(
    skip_ref, rows_ref, kv_ref, query_ref, first_ref, turn_ref, second_ref, out_ref, inner_sum_ref
):
    (convolved,) = inverse(
        [rows_ref[:, :16, :]], first_ref[...], turn_ref[...], second_ref[...]
    )
    inner_sum = convolved + skip_rows(skip_ref) * kv_ref[...].astype(F32)
    inner_sum_ref[...] = inner_sum
    out_ref[...] = (square(query_ref) * inner_sum).astype(BF16)


def skip_rows(table_ref):
    return jnp.concatenate(
        [
            jnp.broadcast_to(table_ref[2 * WEIGHTS + c : 2 * WEIGHTS + c + 1, :], (SIDE, SIDE))
            for c in range(CH)
        ],
        axis=0,
    )


def last_kernel(
    table_ref, rows_ref, inner_ref, key_ref, value_ref, first_ref, turn_ref, second_ref,
    mine_ref, r1_ref, r2_ref, r3_ref,
    out_hbm, grad_key_hbm, grad_value_hbm, grad_taps_hbm,
    out_ref, grad_key_ref, grad_value_ref, grad_taps_ref, sems, *, scale,
):
    copies = []

    def send(src, dst):
        copy = pltpu.make_async_copy(src, dst, sems.at[len(copies)])
        copy.start()
        copies.append(copy)

    both = total_of(mine_ref, (r1_ref, r2_ref, r3_ref))
    out_ref[...] = both.reshape(CH, BLOCK).astype(BF16)
    send(out_ref, out_hbm)
    tables_in = (first_ref[...], turn_ref[...], second_ref[...])
    taps, source = inverse([rows_ref[:, 16:, :], rows_ref[:, :16, :]], *tables_in)
    grad_taps_ref[...] = (taps * scale).reshape(CH, BLOCK)
    send(grad_taps_ref, grad_taps_hbm)
    source = source + skip_rows(table_ref) * inner_ref[...].astype(F32)
    source = source.reshape(CH, BLOCK)
    grad_key_ref[...] = (source * value_ref[...].astype(F32)).astype(BF16)
    send(grad_key_ref, grad_key_hbm)
    grad_value_ref[...] = (source * key_ref[...].astype(F32)).astype(BF16)
    send(grad_value_ref, grad_value_hbm)
    for copy in copies:
        copy.wait()


def call(kernel, outs, operands, scratch=(), place=VMEM, limit=48, cost=None, out_place=VMEM, aliases=None):
    return pl.pallas_call(
        kernel,
        out_shape=[jax.ShapeDtypeStruct(shape, dtype) for shape, dtype in outs],
        in_specs=place if isinstance(place, list) else [place] * len(operands),
        out_specs=out_place if isinstance(out_place, list) else [out_place] * len(outs),
        scratch_shapes=list(scratch),
        input_output_aliases=aliases or {},
        cost_estimate=cost,
        compiler_params=pltpu.CompilerParams(vmem_limit_bytes=limit * 1024 * 1024),
    )(*operands)


def exchange(blocks):
    return lax.all_to_all(blocks, "seq", split_axis=0, concat_axis=0, tiled=True)


def along_y(arrays):
    received = []
    for shift, array in enumerate(arrays, 1):
        pairs = [
            (near * RING + line, near * RING + (line + shift) % RING)
            for near in range(GROUP // RING)
            for line in range(RING)
        ]
        received.append(lax.ppermute(array, "tensor", pairs))
    return received


def across(array):
    return lax.ppermute(array, "tensor", [(i, (i + RING) % GROUP) for i in range(GROUP)])


def body(queries, key_feats, value_feats, filter_taps, skip_gain, out_weight, out_grad):
    first, first_t, turn, second = tables()
    forward_tables = (first, turn, second)
    inverse_tables = (first_t, turn, second)
    square_shape = (ROWS, SIDE)
    tokens = (CH, BLOCK)
    one, two = (BLOCKS, 16, SIDE), (BLOCKS, 32, SIDE)
    parts = [(square_shape, F32)] + [(square_shape, BF16)] * (RING - 1)

    first_inputs = (key_feats, value_feats, filter_taps, out_weight, skip_gain, *forward_tables)
    first_inputs = [
        pltpu.with_memory_space_constraint(array, pltpu.HBM) for array in first_inputs
    ]

    table, key_value, spec = call(
        source_kernel,
        [((2 * WEIGHTS + 8, SIDE), F32), (square_shape, BF16), (two, BF16)],
        first_inputs,
        scratch=[
            *[pltpu.VMEM(tokens, BF16)] * 3,
            pltpu.VMEM(out_weight.shape, BF16),
            pltpu.SMEM((CH,), F32),
            *[pltpu.VMEM(array.shape, array.dtype) for array in forward_tables],
            pltpu.VMEM((2, *one), BF16),
            pltpu.SemaphoreType.DMA((len(first_inputs) + 2,)),
        ],
        place=HBM,
        limit=32,
        out_place=[VMEM, VMEM, ANY],
    )
    spec, far = lax.optimization_barrier((spec, out_grad))
    far = across(far)
    spec = exchange(spec)
    mine, *others = call(
        grad_mix_kernel,
        parts,
        (table, out_grad, far),
        scratch=[pltpu.VMEM(square_shape, F32)] * 2,
        cost=COST,
    )
    others = along_y(others)
    grad_gated, grad_inner, grad_spec = call(
        grad_kernel,
        [(square_shape, F32), (square_shape, BF16), (one, BF16)],
        (mine, *others, queries, *forward_tables),
    )
    (rows,) = call(
        convolve_kernel,
        [(two, BF16)],
        (spec, grad_spec),
        scratch=[pltpu.VMEM((2, 2, BLOCKS, PIECE, SIDE), F32)],
    )
    rows = exchange(rows)
    gated, inner_sum = call(
        gate_kernel,
        [(square_shape, BF16), (square_shape, F32)],
        (table, rows, key_value, queries, *inverse_tables),
    )

    def correlations(half, *given):
        return call(
            functools.partial(correlate_kernel, half),
            [(two, BF16), (tokens, BF16)],
            (spec, rows, inner_sum, grad_gated, *given),
            scratch=[
                pltpu.VMEM((3, 2, BLOCKS, PIECE, SIDE), F32),
                pltpu.VMEM((2, *one), BF16),
                pltpu.VMEM(tokens, BF16),
                pltpu.SemaphoreType.DMA((3,)),
            ],
            place=[VMEM] * 4 + [ANY] * len(given),
            out_place=ANY,
            aliases={4 + i: i for i in range(len(given))},
        )

    *begun, gated = lax.optimization_barrier((*correlations(0), gated))
    far = across(gated)
    corr, grad_queries = correlations(1, *begun)
    corr = exchange(corr)
    mine, *others = call(out_mix_kernel, parts, (table, gated, far), cost=COST)
    others = along_y(others)

    def last(*refs):
        last_kernel(*refs, scale=(BLOCKS * BLOCK) ** -0.5)

    output, grad_keys, grad_values, grad_taps = call(
        last,
        [(tokens, BF16), (tokens, BF16), (tokens, BF16), (tokens, F32)],
        (table, corr, grad_inner, key_feats, value_feats, *inverse_tables, mine, *others),
        scratch=[
            *[pltpu.VMEM(tokens, BF16)] * 3,
            pltpu.VMEM(tokens, F32),
            pltpu.SemaphoreType.DMA((4,)),
        ],
        out_place=ANY,
    )
    return (output, grad_queries, grad_keys, grad_values, grad_taps)


def solution(mesh):
    assert dict(mesh.shape) == {"tensor": GROUP, "seq": BLOCKS}
    placed = P("tensor", "seq")
    return jax.shard_map(
        body,
        mesh=mesh,
        in_specs=(placed, placed, placed, placed, P("tensor"), P(), placed),
        out_specs=(placed,) * 5,
        check_vma=False,
    )
```

```python
import jax
import jax.numpy as jnp
import numpy as np
from jax import lax
from jax.experimental import pallas as pl
from jax.experimental.pallas import tpu as pltpu
from jax.sharding import PartitionSpec as P

F32 = jnp.float32
BF16 = jnp.bfloat16
CH = 2
GROUP = 8
RING = 4
CHUNK = 16
WEIGHTS = RING * CH * 2 * CH
TILE = 4
ORDER = (
    19, 23, 29, 26, 5, 17, 30, 10, 25, 16, 0, 3, 4, 14, 22, 6,
    24, 8, 13, 21, 18, 27, 15, 31, 20, 12, 1, 2, 9, 11, 28, 7,
)
PLACE = tuple(ORDER.index(block) for block in range(len(ORDER)))
BLOCKS = 32
SIDE = 128
ROWS = CH * SIDE
BLOCK = SIDE * SIDE
LENGTH = 2 * BLOCK
PIECE = ROWS // BLOCKS
VMEM = pl.BlockSpec(memory_space=pltpu.VMEM)
COST = pl.CostEstimate(flops=10000000000, bytes_accessed=1000000, transcendentals=0)
HBM = pl.BlockSpec(memory_space=pltpu.HBM)
ANY = pl.BlockSpec(memory_space=pl.ANY)


def tables():
    side = np.arange(SIDE)
    angle = 2 * np.pi * (side[:, None] + 0.5) * side[None, :] / (2 * SIDE)
    first = np.concatenate([np.cos(angle), -np.sin(angle)], axis=0)
    angle = 2 * np.pi * (side[:, None] + 0.5) * side[None, :] / LENGTH
    turn = np.stack([np.cos(angle), np.sin(angle)])
    angle = 2 * np.pi * side[:, None] * side[None, :] / SIDE
    second = np.stack([np.cos(angle), np.sin(angle)])
    return (
        jnp.asarray(first, BF16),
        jnp.asarray(first.T, BF16),
        jnp.asarray(turn, F32),
        jnp.asarray(second, BF16),
    )


def square(ref):
    return ref[...].astype(F32).reshape(ROWS, SIDE)


def second_stage(second, sign):
    cos, sin = second[0], second[1]
    top = [cos, sin] if sign > 0 else [cos, -sin]
    low = [-sin, cos] if sign > 0 else [sin, cos]
    return jnp.concatenate(
        [jnp.concatenate(top, axis=1), jnp.concatenate(low, axis=1)], axis=0
    )


def first_stage(signals, first):
    both = [signal[c * SIDE : (c + 1) * SIDE] for signal in signals for c in range(CH)]
    return jnp.dot(first, jnp.concatenate(both, axis=1), preferred_element_type=F32)


def last_stage(stages, turn, matrix):
    cos, sin = turn[0], turn[1]
    turned = []
    for c in range(CH):
        real, imag = (
            stages[p * SIDE : (p + 1) * SIDE, c * SIDE : (c + 1) * SIDE] for p in (0, 1)
        )
        turned.append(
            jnp.concatenate(
                [(real * cos + imag * sin).astype(BF16), (imag * cos - real * sin).astype(BF16)],
                axis=1,
            )
        )
    spec = jnp.dot(jnp.concatenate(turned, axis=0), matrix, preferred_element_type=F32)
    parts = [spec[:, p * SIDE : (p + 1) * SIDE].reshape(BLOCKS, PIECE, SIDE) for p in (0, 1)]
    return jnp.concatenate(parts, axis=1).astype(BF16)


def inverse(spec, count, first_t, turn, second):
    stages = jnp.dot(spec, second_stage(second, 1), preferred_element_type=F32)
    stages = stages.reshape(BLOCKS, count, PIECE, 2 * SIDE)
    cos, sin = turn[0], turn[1]
    turned = []
    for sig in range(count):
        for c in range(CH):
            owners = slice(c * BLOCKS // CH, (c + 1) * BLOCKS // CH)
            rows = stages[owners, sig].reshape(SIDE, 2 * SIDE)
            real, imag = rows[:, :SIDE], rows[:, SIDE:]
            turned.append(
                jnp.concatenate(
                    [
                        (real * cos - imag * sin).astype(BF16),
                        (imag * cos + real * sin).astype(BF16),
                    ],
                    axis=0,
                )
            )
    both = jnp.dot(first_t, jnp.concatenate(turned, axis=1), preferred_element_type=F32)
    both = both * (2.0 / LENGTH)
    columns = [both[:, c * SIDE : (c + 1) * SIDE] for c in range(CH * count)]
    return [jnp.concatenate(columns[CH * i : CH * i + CH], axis=0) for i in range(count)]


def source_kernel(
    key_hbm, value_hbm, taps_hbm, weight_hbm, skip_hbm, first_hbm, turn_hbm, second_hbm,
    table_ref, kv_ref, spec_hbm,
    key_ref, value_ref, taps_ref, weight_ref, skip_ref, first_ref, turn_ref, second_ref,
    spec_ref, sems,
):
    copies = []

    def send(src, dst):
        copy = pltpu.make_async_copy(src, dst, sems.at[len(copies)])
        copy.start()
        copies.append(copy)

    send(weight_hbm, weight_ref)
    send(skip_hbm, skip_ref)
    send(key_hbm, key_ref)
    send(value_hbm, value_ref)
    send(taps_hbm, taps_ref)
    send(first_hbm, first_ref)
    send(turn_hbm, turn_ref)
    send(second_hbm, second_ref)
    for copy in copies[:2]:
        copy.wait()
    table_ref[:WEIGHTS, :] = weight_rows(weight_ref[...], True)
    table_ref[WEIGHTS : 2 * WEIGHTS, :] = weight_rows(weight_ref[...], False)
    row = lax.broadcasted_iota(jnp.int32, (8, SIDE), 0)
    table_ref[2 * WEIGHTS :, :] = jnp.where(row == 0, skip_ref[0], skip_ref[1])
    for copy in copies[2:6]:
        copy.wait()
    key_value = (square(key_ref) * square(value_ref)).astype(BF16)
    kv_ref[...] = key_value
    stages = first_stage([key_value, square(taps_ref).astype(BF16)], first_ref[...])
    for copy in copies[6:]:
        copy.wait()
    matrix = second_stage(second_ref[...], -1)
    for sig in range(2):
        columns = stages[:, sig * ROWS : (sig + 1) * ROWS]
        spec_ref[:, 16 * sig : 16 * sig + 16, :] = last_stage(columns, turn_ref[...], matrix)
    send(spec_ref, spec_hbm)
    for copy in copies[8:]:
        copy.wait()


def weight_rows(weight, by_row):
    place = lax.axis_index("tensor")
    near, line = place // RING, place % RING
    shape = (WEIGHTS, CH * GROUP)
    row = lax.broadcasted_iota(jnp.int32, shape, 0)
    column = lax.broadcasted_iota(jnp.int32, shape, 1)
    shift, chan, half, i = row // 8, row // 4 % 2, row // 2 % 2, row % 2
    to = (near * RING + (line + shift) % RING) * CH + chan
    of = ((near ^ half) * RING + line) * CH + i
    first, last = (to, of) if by_row else (of, to)
    pick = jnp.where(column == first, 1.0, 0.0).astype(BF16)
    picked = jnp.dot(pick, weight, preferred_element_type=F32)
    value = jnp.sum(jnp.where(column == last, picked, 0.0), axis=1, keepdims=True)
    return jnp.broadcast_to(value, (WEIGHTS, SIDE))


def mix_parts(table_ref, first_row, pieces, mine_ref, other_refs):
    for base in range(0, SIDE, CHUNK):
        loaded = [
            piece[i * SIDE + base : i * SIDE + base + CHUNK, :].astype(F32)
            for piece in pieces
            for i in range(CH)
        ]
        for shift in range(RING):
            for c in range(CH):
                total = None
                for i, value in enumerate(loaded):
                    row = first_row + (shift * CH + c) * 4 + i
                    part = table_ref[row : row + 1, :] * value
                    total = part if total is None else total + part
                place_rows = pl.ds(c * SIDE + base, CHUNK)
                if shift == 0:
                    mine_ref[place_rows, :] = total
                else:
                    other_refs[shift - 1][place_rows, :] = total.astype(BF16)


def grad_mix_kernel(table_ref, near_ref, far_ref, mine_ref, *rest):
    other_refs, squares = rest[: RING - 1], rest[RING - 1 :]
    for ref, buf in zip((near_ref, far_ref), squares):
        buf[...] = square(ref)
    mix_parts(table_ref, 0, squares, mine_ref, other_refs)


def out_mix_kernel(table_ref, near_ref, far_ref, mine_ref, *other_refs):
    mix_parts(table_ref, WEIGHTS, (near_ref, far_ref), mine_ref, other_refs)


def total_of(mine_ref, other_refs):
    total = mine_ref[...]
    for ref in other_refs:
        total = total + ref[...].astype(F32)
    return total


def load(spec_ref, sig, buf_ref, slot):
    both = spec_ref[:, 16 * sig : 16 * sig + 16, :].astype(F32)
    buf_ref[slot, 0] = both[:, :PIECE]
    buf_ref[slot, 1] = both[:, PIECE:]


def alternate():
    row = lax.broadcasted_iota(jnp.int32, (PIECE, SIDE), 0)
    return jnp.where(row % 2 == 0, 1.0, -1.0).astype(F32)


def put(out_ref, blk, sig, real, imag):
    both = jnp.concatenate([real, imag], axis=0)
    out_ref[PLACE[blk], 16 * sig : 16 * sig + 16, :] = both.astype(BF16)


def add(total, parts):
    return parts if total is None else tuple(t + p for t, p in zip(total, parts))


def convolve(buf_ref, out_ref, sign):
    def at(slot, blk):
        return buf_ref[slot, 0, PLACE[blk]], buf_ref[slot, 1, PLACE[blk]]

    last = None
    for base in range(0, BLOCKS, TILE):
        sums = [None] * TILE
        window = {}
        for j in range(base + TILE):
            hr, hi = at(1, j)
            plus, minus = hr + hi, hi - hr
            for o in range(TILE):
                blk = base + o - j
                if blk < 0:
                    continue
                if blk not in window:
                    xr, xi = at(0, blk)
                    window[blk] = (xr, xi, xr + xi)
                xr, xi, both = window[blk]
                sums[o] = add(sums[o], (hr * both, xi * plus, xr * minus))
        for o in range(TILE):
            common, of_real, of_imag = sums[o]
            total = (common - of_real, common + of_imag)
            real, imag = total
            if last is not None:
                real, imag = real - sign * last[1], imag + sign * last[0]
            put(out_ref, base + o, 0, real, imag)
            last = total


def correlate(buf_ref, loaded_ref, out_ref, sign):
    def at(ref, slot, blk):
        return ref[slot, 0, PLACE[blk]], ref[slot, 1, PLACE[blk]]

    after = [None, None]
    for base in range(BLOCKS - TILE, -1, -TILE):
        rows = [[None, None] for _ in range(TILE)]
        for sig, other in ((0, 1), (1, 0)):
            sums = [None] * TILE
            window = {}
            for j in range(BLOCKS - base):
                hr, hi = at(loaded_ref, other, j)
                plus, minus = hr + hi, hr - hi
                for o in range(TILE):
                    blk = base + o + j
                    if blk >= BLOCKS:
                        continue
                    if blk not in window:
                        gr, gi = at(buf_ref, 0, blk)
                        window[blk] = (gr, gi, gr + gi)
                    gr, gi, both = window[blk]
                    sums[o] = add(sums[o], (hr * both, gi * minus, gr * plus))
            for o in range(TILE - 1, -1, -1):
                common, of_real, of_imag = sums[o]
                total = (common - of_real, common - of_imag)
                real, imag = total
                if after[sig] is not None:
                    real, imag = real + sign * after[sig][1], imag - sign * after[sig][0]
                rows[o][sig] = (real, imag)
                after[sig] = total
        for o in range(TILE):
            for p in range(2):
                put(out_ref, base + o, p, rows[o][0][p], rows[o][1][p])


def convolve_kernel(spec_ref, grad_ref, out_ref, buf_ref):
    out_ref[:, 16:, :] = grad_ref[...]
    load(spec_ref, 0, buf_ref, 0)
    load(spec_ref, 1, buf_ref, 1)
    convolve(buf_ref, out_ref, alternate())


def grad_kernel(
    mine_ref, r1_ref, r2_ref, r3_ref, query_ref, first_ref, turn_ref, second_ref,
    gated_ref, inner_ref, out_ref,
):
    grad_gated = total_of(mine_ref, (r1_ref, r2_ref, r3_ref))
    gated_ref[...] = grad_gated
    grad_inner = (grad_gated * square(query_ref)).astype(BF16)
    inner_ref[...] = grad_inner
    stages = first_stage([grad_inner], first_ref[...])
    out_ref[...] = last_stage(stages, turn_ref[...], second_stage(second_ref[...], -1))


def gate(table_ref, rows_ref, kv_ref, query_ref, first_ref, turn_ref, second_ref, out_ref):
    rows = rows_ref[:, :16, :].astype(F32)
    parts = [rows[:, p * PIECE : (p + 1) * PIECE].reshape(ROWS, SIDE).astype(BF16) for p in (0, 1)]
    (convolved,) = inverse(
        jnp.concatenate(parts, axis=1), 1, first_ref[...], turn_ref[...], second_ref[...]
    )
    inner_sum = convolved + skip_rows(table_ref) * kv_ref[...].astype(F32)
    out_ref[...] = (square(query_ref) * inner_sum).astype(BF16)
    return inner_sum


def correlations(
    loaded_ref, rows_ref, inner_sum, gated_ref, out_hbm, grad_query_hbm,
    buf_ref, out_ref, grad_query_ref, sems,
):
    grad_query_ref[...] = (gated_ref[...] * inner_sum).reshape(CH, BLOCK).astype(BF16)
    query_copy = pltpu.make_async_copy(grad_query_ref, grad_query_hbm, sems.at[0])
    query_copy.start()
    load(rows_ref, 1, buf_ref, 0)
    sign = alternate()
    correlate(buf_ref, loaded_ref, out_ref, sign)
    copy = pltpu.make_async_copy(out_ref, out_hbm, sems.at[1])
    copy.start()
    copy.wait()
    query_copy.wait()


def near_kernel(
    table_ref, rows_ref, kv_ref, query_ref, first_ref, turn_ref, second_ref, loaded_ref, gated_ref,
    gated_out_ref, inner_sum_ref, out_hbm, grad_query_hbm, *scratch,
):
    gate_refs = (
        table_ref, rows_ref, kv_ref, query_ref, first_ref, turn_ref, second_ref, gated_out_ref
    )
    near = lax.axis_index("tensor") // RING == 0

    @pl.when(near)
    def _():
        inner_sum = gate(*gate_refs)
        correlations(
            loaded_ref, rows_ref, inner_sum, gated_ref, out_hbm, grad_query_hbm, *scratch
        )

    @pl.when(jnp.logical_not(near))
    def _():
        inner_sum_ref[...] = gate(*gate_refs)


def far_kernel(
    loaded_ref, rows_ref, inner_sum_ref, gated_ref, _, __, out_hbm, grad_query_hbm, *scratch
):
    @pl.when(lax.axis_index("tensor") // RING == 1)
    def _():
        correlations(
            loaded_ref, rows_ref, inner_sum_ref[...], gated_ref, out_hbm, grad_query_hbm, *scratch
        )


def skip_rows(table_ref):
    return jnp.concatenate(
        [
            jnp.broadcast_to(table_ref[2 * WEIGHTS + c : 2 * WEIGHTS + c + 1, :], (SIDE, SIDE))
            for c in range(CH)
        ],
        axis=0,
    )


def last_kernel(
    table_ref, rows_ref, inner_ref, key_ref, value_ref, first_ref, turn_ref, second_ref,
    mine_ref, r1_ref, r2_ref, r3_ref,
    out_hbm, grad_key_hbm, grad_value_hbm, grad_taps_hbm,
    out_ref, grad_key_ref, grad_value_ref, grad_taps_ref, sems, *, scale,
):
    copies = []

    def send(src, dst):
        copy = pltpu.make_async_copy(src, dst, sems.at[len(copies)])
        copy.start()
        copies.append(copy)

    both = total_of(mine_ref, (r1_ref, r2_ref, r3_ref))
    out_ref[...] = both.reshape(CH, BLOCK).astype(BF16)
    send(out_ref, out_hbm)
    tables_in = (first_ref[...], turn_ref[...], second_ref[...])
    parts = [rows_ref[:, 16 * p : 16 * p + 16, :].reshape(2 * ROWS, SIDE) for p in (0, 1)]
    source, taps = inverse(jnp.concatenate(parts, axis=1), 2, *tables_in)
    grad_taps_ref[...] = (taps * scale).reshape(CH, BLOCK)
    send(grad_taps_ref, grad_taps_hbm)
    source = source + skip_rows(table_ref) * inner_ref[...].astype(F32)
    source = source.reshape(CH, BLOCK)
    grad_key_ref[...] = (source * value_ref[...].astype(F32)).astype(BF16)
    send(grad_key_ref, grad_key_hbm)
    grad_value_ref[...] = (source * key_ref[...].astype(F32)).astype(BF16)
    send(grad_value_ref, grad_value_hbm)
    for copy in copies:
        copy.wait()


def call(kernel, outs, operands, scratch=(), place=VMEM, limit=48, cost=None, out_place=VMEM, aliases=None):
    return pl.pallas_call(
        kernel,
        out_shape=[jax.ShapeDtypeStruct(shape, dtype) for shape, dtype in outs],
        in_specs=place if isinstance(place, list) else [place] * len(operands),
        out_specs=out_place if isinstance(out_place, list) else [out_place] * len(outs),
        scratch_shapes=list(scratch),
        input_output_aliases=aliases or {},
        cost_estimate=cost,
        compiler_params=pltpu.CompilerParams(vmem_limit_bytes=limit * 1024 * 1024),
    )(*operands)


def exchange(blocks):
    return lax.all_to_all(
        blocks, "seq", split_axis=0, concat_axis=0, tiled=True, axis_index_groups=[list(ORDER)]
    )


def along_y(arrays):
    received = []
    for shift, array in enumerate(arrays, 1):
        pairs = [
            (near * RING + line, near * RING + (line + shift) % RING)
            for near in range(GROUP // RING)
            for line in range(RING)
        ]
        received.append(lax.ppermute(array, "tensor", pairs))
    return received


def across(array):
    return lax.ppermute(array, "tensor", [(i, (i + RING) % GROUP) for i in range(GROUP)])


def body(queries, key_feats, value_feats, filter_taps, skip_gain, out_weight, out_grad):
    first, first_t, turn, second = tables()
    forward_tables = (first, turn, second)
    inverse_tables = (first_t, turn, second)
    square_shape = (ROWS, SIDE)
    tokens = (CH, BLOCK)
    one, two = (BLOCKS, 16, SIDE), (BLOCKS, 32, SIDE)
    parts = [(square_shape, F32)] + [(square_shape, BF16)] * (RING - 1)

    first_inputs = (key_feats, value_feats, filter_taps, out_weight, skip_gain, *forward_tables)
    first_inputs = [
        pltpu.with_memory_space_constraint(array, pltpu.HBM) for array in first_inputs
    ]

    table, key_value, spec = call(
        source_kernel,
        [((2 * WEIGHTS + 8, SIDE), F32), (square_shape, BF16), (two, BF16)],
        first_inputs,
        scratch=[
            *[pltpu.VMEM(tokens, BF16)] * 3,
            pltpu.VMEM(out_weight.shape, BF16),
            pltpu.SMEM((CH,), F32),
            *[pltpu.VMEM(array.shape, array.dtype) for array in forward_tables],
            pltpu.VMEM(two, BF16),
            pltpu.SemaphoreType.DMA((len(first_inputs) + 1,)),
        ],
        place=HBM,
        limit=32,
        out_place=[VMEM, VMEM, ANY],
    )
    spec, far = lax.optimization_barrier((spec, out_grad))
    far = across(far)
    spec = exchange(spec)
    mine, *others = call(
        grad_mix_kernel,
        parts,
        (table, out_grad, far),
        scratch=[pltpu.VMEM(square_shape, F32)] * 2,
        cost=COST,
    )
    others = along_y(others)
    grad_gated, grad_inner, grad_spec = call(
        grad_kernel,
        [(square_shape, F32), (square_shape, BF16), (one, BF16)],
        (mine, *others, queries, *forward_tables),
    )
    rows, loaded = call(
        convolve_kernel,
        [(two, BF16), ((2, 2, BLOCKS, PIECE, SIDE), F32)],
        (spec, grad_spec),
    )
    rows = exchange(rows)
    scratch = [
        pltpu.VMEM((1, 2, BLOCKS, PIECE, SIDE), F32),
        pltpu.VMEM(two, BF16),
        pltpu.VMEM(tokens, BF16),
        pltpu.SemaphoreType.DMA((2,)),
    ]
    gated, inner_sum, *begun = call(
        near_kernel,
        [(square_shape, BF16), (square_shape, F32), (two, BF16), (tokens, BF16)],
        (table, rows, key_value, queries, *inverse_tables, loaded, grad_gated),
        scratch=scratch,
        out_place=[VMEM, VMEM, ANY, ANY],
    )
    far = across(gated)
    corr, grad_queries = call(
        far_kernel,
        [(two, BF16), (tokens, BF16)],
        (loaded, rows, inner_sum, grad_gated, *begun),
        scratch=scratch,
        place=[VMEM] * 4 + [ANY] * 2,
        out_place=ANY,
        aliases={4: 0, 5: 1},
    )
    corr = exchange(corr)
    mine, *others = call(out_mix_kernel, parts, (table, gated, far), cost=COST)
    others = along_y(others)

    def last(*refs):
        last_kernel(*refs, scale=(BLOCKS * BLOCK) ** -0.5)

    output, grad_keys, grad_values, grad_taps = call(
        last,
        [(tokens, BF16), (tokens, BF16), (tokens, BF16), (tokens, F32)],
        (table, corr, grad_inner, key_feats, value_feats, *inverse_tables, mine, *others),
        scratch=[
            *[pltpu.VMEM(tokens, BF16)] * 3,
            pltpu.VMEM(tokens, F32),
            pltpu.SemaphoreType.DMA((4,)),
        ],
        out_place=ANY,
    )
    return (output, grad_queries, grad_keys, grad_values, grad_taps)


def solution(mesh):
    assert dict(mesh.shape) == {"tensor": GROUP, "seq": BLOCKS}
    placed = P("tensor", "seq")
    return jax.shard_map(
        body,
        mesh=mesh,
        in_specs=(placed, placed, placed, placed, P("tensor"), P(), placed),
        out_specs=(placed,) * 5,
        check_vma=False,
    )
```

```python
import jax
import jax.numpy as jnp
import numpy as np
from jax import lax
from jax.experimental import pallas as pl
from jax.experimental.pallas import tpu as pltpu
from jax.sharding import PartitionSpec as P

F32 = jnp.float32
BF16 = jnp.bfloat16
CH = 2
GROUP = 8
RING = 4
CHUNK = 16
WEIGHTS = RING * CH * 2 * CH
TILE = 4
ORDER = (
    19, 23, 29, 26, 5, 17, 30, 10, 25, 16, 0, 3, 4, 14, 22, 6,
    24, 8, 13, 21, 18, 27, 15, 31, 20, 12, 1, 2, 9, 11, 28, 7,
)
PLACE = tuple(ORDER.index(block) for block in range(len(ORDER)))
BLOCKS = 32
SIDE = 128
ROWS = CH * SIDE
BLOCK = SIDE * SIDE
LENGTH = 2 * BLOCK
PIECE = ROWS // BLOCKS
VMEM = pl.BlockSpec(memory_space=pltpu.VMEM)
COST = pl.CostEstimate(flops=10000000000, bytes_accessed=1000000, transcendentals=0)
HBM = pl.BlockSpec(memory_space=pltpu.HBM)
ANY = pl.BlockSpec(memory_space=pl.ANY)


def tables():
    side = np.arange(SIDE)
    angle = 2 * np.pi * (side[:, None] + 0.5) * side[None, :] / (2 * SIDE)
    first = np.concatenate([np.cos(angle), -np.sin(angle)], axis=0)
    angle = 2 * np.pi * (side[:, None] + 0.5) * side[None, :] / LENGTH
    turn = np.stack([np.cos(angle), np.sin(angle)])
    angle = 2 * np.pi * side[:, None] * side[None, :] / SIDE
    second = np.stack([np.cos(angle), np.sin(angle)])
    return (
        jnp.asarray(first, BF16),
        jnp.asarray(first.T, BF16),
        jnp.asarray(turn, F32),
        jnp.asarray(second, BF16),
    )


def square(ref):
    return ref[...].astype(F32).reshape(ROWS, SIDE)


def second_stage(second, sign):
    cos, sin = second[0], second[1]
    top = [cos, sin] if sign > 0 else [cos, -sin]
    low = [-sin, cos] if sign > 0 else [sin, cos]
    return jnp.concatenate(
        [jnp.concatenate(top, axis=1), jnp.concatenate(low, axis=1)], axis=0
    )


def first_stage(signals, first):
    both = [signal[c * SIDE : (c + 1) * SIDE] for signal in signals for c in range(CH)]
    return jnp.dot(first, jnp.concatenate(both, axis=1), preferred_element_type=F32)


def last_stage(stages, turn, matrix):
    cos, sin = turn[0], turn[1]
    turned = []
    for c in range(CH):
        real, imag = (
            stages[p * SIDE : (p + 1) * SIDE, c * SIDE : (c + 1) * SIDE] for p in (0, 1)
        )
        turned.append(
            jnp.concatenate(
                [(real * cos + imag * sin).astype(BF16), (imag * cos - real * sin).astype(BF16)],
                axis=1,
            )
        )
    spec = jnp.dot(jnp.concatenate(turned, axis=0), matrix, preferred_element_type=F32)
    parts = [spec[:, p * SIDE : (p + 1) * SIDE].reshape(BLOCKS, PIECE, SIDE) for p in (0, 1)]
    return jnp.concatenate(parts, axis=1).astype(BF16)


def inverse(spec, count, first_t, turn, second):
    stages = jnp.dot(spec, second_stage(second, 1), preferred_element_type=F32)
    stages = stages.reshape(BLOCKS, count, PIECE, 2 * SIDE)
    cos, sin = turn[0], turn[1]
    turned = []
    for sig in range(count):
        for c in range(CH):
            owners = slice(c * BLOCKS // CH, (c + 1) * BLOCKS // CH)
            rows = stages[owners, sig].reshape(SIDE, 2 * SIDE)
            real, imag = rows[:, :SIDE], rows[:, SIDE:]
            turned.append(
                jnp.concatenate(
                    [
                        (real * cos - imag * sin).astype(BF16),
                        (imag * cos + real * sin).astype(BF16),
                    ],
                    axis=0,
                )
            )
    both = jnp.dot(first_t, jnp.concatenate(turned, axis=1), preferred_element_type=F32)
    both = both * (2.0 / LENGTH)
    columns = [both[:, c * SIDE : (c + 1) * SIDE] for c in range(CH * count)]
    return [jnp.concatenate(columns[CH * i : CH * i + CH], axis=0) for i in range(count)]


def source_kernel(
    key_hbm, value_hbm, taps_hbm, weight_hbm, skip_hbm, first_hbm, turn_hbm, second_hbm,
    table_ref, kv_ref, spec_hbm,
    key_ref, value_ref, taps_ref, weight_ref, skip_ref, first_ref, turn_ref, second_ref,
    spec_ref, sems,
):
    copies = []

    def send(src, dst):
        copy = pltpu.make_async_copy(src, dst, sems.at[len(copies)])
        copy.start()
        copies.append(copy)

    send(weight_hbm, weight_ref)
    send(skip_hbm, skip_ref)
    send(key_hbm, key_ref)
    send(value_hbm, value_ref)
    send(taps_hbm, taps_ref)
    send(first_hbm, first_ref)
    send(turn_hbm, turn_ref)
    send(second_hbm, second_ref)
    for copy in copies[:2]:
        copy.wait()
    table_ref[:WEIGHTS, :] = weight_rows(weight_ref[...], True)
    table_ref[WEIGHTS : 2 * WEIGHTS, :] = weight_rows(weight_ref[...], False)
    row = lax.broadcasted_iota(jnp.int32, (8, SIDE), 0)
    table_ref[2 * WEIGHTS :, :] = jnp.where(row == 0, skip_ref[0], skip_ref[1])
    for copy in copies[2:6]:
        copy.wait()
    key_value = (square(key_ref) * square(value_ref)).astype(BF16)
    kv_ref[...] = key_value
    stages = first_stage([key_value, square(taps_ref).astype(BF16)], first_ref[...])
    for copy in copies[6:]:
        copy.wait()
    matrix = second_stage(second_ref[...], -1)
    for sig in range(2):
        columns = stages[:, sig * ROWS : (sig + 1) * ROWS]
        spec_ref[:, 16 * sig : 16 * sig + 16, :] = last_stage(columns, turn_ref[...], matrix)
    send(spec_ref, spec_hbm)
    for copy in copies[8:]:
        copy.wait()


def weight_rows(weight, by_row):
    place = lax.axis_index("tensor")
    near, line = place // RING, place % RING
    shape = (WEIGHTS, CH * GROUP)
    row = lax.broadcasted_iota(jnp.int32, shape, 0)
    column = lax.broadcasted_iota(jnp.int32, shape, 1)
    shift, chan, half, i = row // 8, row // 4 % 2, row // 2 % 2, row % 2
    to = (near * RING + (line + shift) % RING) * CH + chan
    of = ((near ^ half) * RING + line) * CH + i
    first, last = (to, of) if by_row else (of, to)
    pick = jnp.where(column == first, 1.0, 0.0).astype(BF16)
    picked = jnp.dot(pick, weight, preferred_element_type=F32)
    value = jnp.sum(jnp.where(column == last, picked, 0.0), axis=1, keepdims=True)
    return jnp.broadcast_to(value, (WEIGHTS, SIDE))


def mix_parts(table_ref, first_row, pieces, mine_ref, other_refs):
    for base in range(0, SIDE, CHUNK):
        loaded = [
            piece[i * SIDE + base : i * SIDE + base + CHUNK, :].astype(F32)
            for piece in pieces
            for i in range(CH)
        ]
        for shift in range(RING):
            for c in range(CH):
                total = None
                for i, value in enumerate(loaded):
                    row = first_row + (shift * CH + c) * 4 + i
                    part = table_ref[row : row + 1, :] * value
                    total = part if total is None else total + part
                place_rows = pl.ds(c * SIDE + base, CHUNK)
                if shift == 0:
                    mine_ref[place_rows, :] = total
                else:
                    other_refs[shift - 1][place_rows, :] = total.astype(BF16)


def grad_mix_kernel(table_ref, near_ref, far_ref, mine_ref, *rest):
    other_refs, squares = rest[: RING - 1], rest[RING - 1 :]
    for ref, buf in zip((near_ref, far_ref), squares):
        buf[...] = square(ref)
    mix_parts(table_ref, 0, squares, mine_ref, other_refs)


def out_mix_kernel(table_ref, near_ref, far_ref, mine_ref, *other_refs):
    mix_parts(table_ref, WEIGHTS, (near_ref, far_ref), mine_ref, other_refs)


def total_of(mine_ref, other_refs):
    total = mine_ref[...]
    for ref in other_refs:
        total = total + ref[...].astype(F32)
    return total


def load(spec_ref, sig, buf_ref, slot):
    both = spec_ref[:, 16 * sig : 16 * sig + 16, :].astype(F32)
    buf_ref[slot, 0] = both[:, :PIECE]
    buf_ref[slot, 1] = both[:, PIECE:]


def alternate():
    row = lax.broadcasted_iota(jnp.int32, (PIECE, SIDE), 0)
    return jnp.where(row % 2 == 0, 1.0, -1.0).astype(F32)


def put(out_ref, blk, sig, real, imag):
    both = jnp.concatenate([real, imag], axis=0)
    out_ref[PLACE[blk], 16 * sig : 16 * sig + 16, :] = both.astype(BF16)


def add(total, parts):
    return parts if total is None else tuple(t + p for t, p in zip(total, parts))


def convolve(buf_ref, out_ref, sign):
    def at(slot, blk):
        return buf_ref[slot, 0, PLACE[blk]], buf_ref[slot, 1, PLACE[blk]]

    last = None
    for base in range(0, BLOCKS, TILE):
        sums = [None] * TILE
        window = {}
        for j in range(base + TILE):
            hr, hi = at(1, j)
            plus, minus = hr + hi, hi - hr
            for o in range(TILE):
                blk = base + o - j
                if blk < 0:
                    continue
                if blk not in window:
                    xr, xi = at(0, blk)
                    window[blk] = (xr, xi, xr + xi)
                xr, xi, both = window[blk]
                sums[o] = add(sums[o], (hr * both, xi * plus, xr * minus))
        for o in range(TILE):
            common, of_real, of_imag = sums[o]
            total = (common - of_real, common + of_imag)
            real, imag = total
            if last is not None:
                real, imag = real - sign * last[1], imag + sign * last[0]
            put(out_ref, base + o, 0, real, imag)
            last = total


def correlate(buf_ref, loaded_ref, out_ref, sign):
    def at(ref, slot, blk):
        return ref[slot, 0, PLACE[blk]], ref[slot, 1, PLACE[blk]]

    after = [None, None]
    for base in range(BLOCKS - TILE, -1, -TILE):
        rows = [[None, None] for _ in range(TILE)]
        for sig, other in ((0, 1), (1, 0)):
            sums = [None] * TILE
            window = {}
            for j in range(BLOCKS - base):
                hr, hi = at(loaded_ref, other, j)
                plus, minus = hr + hi, hr - hi
                for o in range(TILE):
                    blk = base + o + j
                    if blk >= BLOCKS:
                        continue
                    if blk not in window:
                        gr, gi = at(buf_ref, 0, blk)
                        window[blk] = (gr, gi, gr + gi)
                    gr, gi, both = window[blk]
                    sums[o] = add(sums[o], (hr * both, gi * minus, gr * plus))
            for o in range(TILE - 1, -1, -1):
                common, of_real, of_imag = sums[o]
                total = (common - of_real, common - of_imag)
                real, imag = total
                if after[sig] is not None:
                    real, imag = real + sign * after[sig][1], imag - sign * after[sig][0]
                rows[o][sig] = (real, imag)
                after[sig] = total
        for o in range(TILE):
            for p in range(2):
                put(out_ref, base + o, p, rows[o][0][p], rows[o][1][p])


def convolve_kernel(spec_ref, grad_ref, out_ref, buf_ref):
    out_ref[:, 16:, :] = grad_ref[...]
    load(spec_ref, 0, buf_ref, 0)
    load(spec_ref, 1, buf_ref, 1)
    convolve(buf_ref, out_ref, alternate())


def grad_kernel(
    mine_ref, r1_ref, r2_ref, r3_ref, query_ref, first_ref, turn_ref, second_ref,
    gated_ref, inner_ref, out_ref,
):
    grad_gated = total_of(mine_ref, (r1_ref, r2_ref, r3_ref))
    gated_ref[...] = grad_gated
    grad_inner = (grad_gated * square(query_ref)).astype(BF16)
    inner_ref[...] = grad_inner
    stages = first_stage([grad_inner], first_ref[...])
    out_ref[...] = last_stage(stages, turn_ref[...], second_stage(second_ref[...], -1))


def gate(table_ref, rows_ref, kv_ref, query_ref, first_ref, turn_ref, second_ref, out_ref):
    rows = rows_ref[:, :16, :].astype(F32)
    parts = [rows[:, p * PIECE : (p + 1) * PIECE].reshape(ROWS, SIDE).astype(BF16) for p in (0, 1)]
    (convolved,) = inverse(
        jnp.concatenate(parts, axis=1), 1, first_ref[...], turn_ref[...], second_ref[...]
    )
    inner_sum = convolved + skip_rows(table_ref) * kv_ref[...].astype(F32)
    out_ref[...] = (square(query_ref) * inner_sum).astype(BF16)
    return inner_sum


def near_kernel(
    table_ref, rows_ref, kv_ref, query_ref, first_ref, turn_ref, second_ref, loaded_ref, gated_ref,
    gated_out_ref, inner_sum_ref, out_ref, grad_query_ref, buf_ref,
):
    gate_refs = (
        table_ref, rows_ref, kv_ref, query_ref, first_ref, turn_ref, second_ref, gated_out_ref
    )
    near = lax.axis_index("tensor") // RING == 0

    @pl.when(near)
    def _():
        inner_sum = gate(*gate_refs)
        grad_query_ref[...] = (gated_ref[...] * inner_sum).reshape(CH, BLOCK).astype(BF16)
        load(rows_ref, 1, buf_ref, 0)
        correlate(buf_ref, loaded_ref, out_ref, alternate())

    @pl.when(jnp.logical_not(near))
    def _():
        inner_sum_ref[...] = gate(*gate_refs)


def far_kernel(
    loaded_ref, rows_ref, inner_sum_ref, gated_ref, near_ref, near_query_ref,
    out_hbm, grad_query_hbm, buf_ref, out_ref, grad_query_ref, sems,
):
    near = lax.axis_index("tensor") // RING == 0

    @pl.when(near)
    def _():
        copies = [
            pltpu.make_async_copy(near_ref, out_hbm, sems.at[0]),
            pltpu.make_async_copy(near_query_ref, grad_query_hbm, sems.at[1]),
        ]
        for copy in copies:
            copy.start()
        for copy in copies:
            copy.wait()

    @pl.when(jnp.logical_not(near))
    def _():
        grad_query_ref[...] = (
            (gated_ref[...] * inner_sum_ref[...]).reshape(CH, BLOCK).astype(BF16)
        )
        copies = [pltpu.make_async_copy(grad_query_ref, grad_query_hbm, sems.at[0])]
        copies[0].start()
        load(rows_ref, 1, buf_ref, 0)
        correlate(buf_ref, loaded_ref, out_ref, alternate())
        copies.append(pltpu.make_async_copy(out_ref, out_hbm, sems.at[1]))
        copies[1].start()
        for copy in copies:
            copy.wait()


def skip_rows(table_ref):
    return jnp.concatenate(
        [
            jnp.broadcast_to(table_ref[2 * WEIGHTS + c : 2 * WEIGHTS + c + 1, :], (SIDE, SIDE))
            for c in range(CH)
        ],
        axis=0,
    )


def last_kernel(
    table_ref, rows_ref, inner_ref, key_ref, value_ref, first_ref, turn_ref, second_ref,
    mine_ref, r1_ref, r2_ref, r3_ref,
    out_hbm, grad_key_hbm, grad_value_hbm, grad_taps_hbm,
    out_ref, grad_key_ref, grad_value_ref, grad_taps_ref, sems, *, scale,
):
    copies = []

    def send(src, dst):
        copy = pltpu.make_async_copy(src, dst, sems.at[len(copies)])
        copy.start()
        copies.append(copy)

    both = total_of(mine_ref, (r1_ref, r2_ref, r3_ref))
    out_ref[...] = both.reshape(CH, BLOCK).astype(BF16)
    send(out_ref, out_hbm)
    tables_in = (first_ref[...], turn_ref[...], second_ref[...])
    parts = [rows_ref[:, 16 * p : 16 * p + 16, :].reshape(2 * ROWS, SIDE) for p in (0, 1)]
    source, taps = inverse(jnp.concatenate(parts, axis=1), 2, *tables_in)
    grad_taps_ref[...] = (taps * scale).reshape(CH, BLOCK)
    send(grad_taps_ref, grad_taps_hbm)
    source = source + skip_rows(table_ref) * inner_ref[...].astype(F32)
    source = source.reshape(CH, BLOCK)
    grad_key_ref[...] = (source * value_ref[...].astype(F32)).astype(BF16)
    send(grad_key_ref, grad_key_hbm)
    grad_value_ref[...] = (source * key_ref[...].astype(F32)).astype(BF16)
    send(grad_value_ref, grad_value_hbm)
    for copy in copies:
        copy.wait()


def call(kernel, outs, operands, scratch=(), place=VMEM, limit=48, cost=None, out_place=VMEM):
    return pl.pallas_call(
        kernel,
        out_shape=[jax.ShapeDtypeStruct(shape, dtype) for shape, dtype in outs],
        in_specs=place if isinstance(place, list) else [place] * len(operands),
        out_specs=out_place if isinstance(out_place, list) else [out_place] * len(outs),
        scratch_shapes=list(scratch),
        cost_estimate=cost,
        compiler_params=pltpu.CompilerParams(vmem_limit_bytes=limit * 1024 * 1024),
    )(*operands)


def exchange(blocks):
    return lax.all_to_all(
        blocks, "seq", split_axis=0, concat_axis=0, tiled=True, axis_index_groups=[list(ORDER)]
    )


def along_y(arrays):
    received = []
    for shift, array in enumerate(arrays, 1):
        pairs = [
            (near * RING + line, near * RING + (line + shift) % RING)
            for near in range(GROUP // RING)
            for line in range(RING)
        ]
        received.append(lax.ppermute(array, "tensor", pairs))
    return received


def across(array):
    return lax.ppermute(array, "tensor", [(i, (i + RING) % GROUP) for i in range(GROUP)])


def body(queries, key_feats, value_feats, filter_taps, skip_gain, out_weight, out_grad):
    first, first_t, turn, second = tables()
    forward_tables = (first, turn, second)
    inverse_tables = (first_t, turn, second)
    square_shape = (ROWS, SIDE)
    tokens = (CH, BLOCK)
    one, two = (BLOCKS, 16, SIDE), (BLOCKS, 32, SIDE)
    parts = [(square_shape, F32)] + [(square_shape, BF16)] * (RING - 1)

    first_inputs = (key_feats, value_feats, filter_taps, out_weight, skip_gain, *forward_tables)
    first_inputs = [
        pltpu.with_memory_space_constraint(array, pltpu.HBM) for array in first_inputs
    ]

    table, key_value, spec = call(
        source_kernel,
        [((2 * WEIGHTS + 8, SIDE), F32), (square_shape, BF16), (two, BF16)],
        first_inputs,
        scratch=[
            *[pltpu.VMEM(tokens, BF16)] * 3,
            pltpu.VMEM(out_weight.shape, BF16),
            pltpu.SMEM((CH,), F32),
            *[pltpu.VMEM(array.shape, array.dtype) for array in forward_tables],
            pltpu.VMEM(two, BF16),
            pltpu.SemaphoreType.DMA((len(first_inputs) + 1,)),
        ],
        place=HBM,
        limit=32,
        out_place=[VMEM, VMEM, ANY],
    )
    spec, far = lax.optimization_barrier((spec, out_grad))
    far = across(far)
    spec = exchange(spec)
    mine, *others = call(
        grad_mix_kernel,
        parts,
        (table, out_grad, far),
        scratch=[pltpu.VMEM(square_shape, F32)] * 2,
        cost=COST,
    )
    others = along_y(others)
    grad_gated, grad_inner, grad_spec = call(
        grad_kernel,
        [(square_shape, F32), (square_shape, BF16), (one, BF16)],
        (mine, *others, queries, *forward_tables),
    )
    rows, loaded = call(
        convolve_kernel,
        [(two, BF16), ((2, 2, BLOCKS, PIECE, SIDE), F32)],
        (spec, grad_spec),
    )
    rows = exchange(rows)
    gated, inner_sum, *begun = call(
        near_kernel,
        [(square_shape, BF16), (square_shape, F32), (two, BF16), (tokens, BF16)],
        (table, rows, key_value, queries, *inverse_tables, loaded, grad_gated),
        scratch=[pltpu.VMEM((1, 2, BLOCKS, PIECE, SIDE), F32)],
    )
    far = across(gated)
    corr, grad_queries = call(
        far_kernel,
        [(two, BF16), (tokens, BF16)],
        (loaded, rows, inner_sum, grad_gated, *begun),
        scratch=[
            pltpu.VMEM((1, 2, BLOCKS, PIECE, SIDE), F32),
            pltpu.VMEM(two, BF16),
            pltpu.VMEM(tokens, BF16),
            pltpu.SemaphoreType.DMA((2,)),
        ],
        out_place=ANY,
    )
    corr = exchange(corr)
    mine, *others = call(out_mix_kernel, parts, (table, gated, far), cost=COST)
    others = along_y(others)

    def last(*refs):
        last_kernel(*refs, scale=(BLOCKS * BLOCK) ** -0.5)

    output, grad_keys, grad_values, grad_taps = call(
        last,
        [(tokens, BF16), (tokens, BF16), (tokens, BF16), (tokens, F32)],
        (table, corr, grad_inner, key_feats, value_feats, *inverse_tables, mine, *others),
        scratch=[
            *[pltpu.VMEM(tokens, BF16)] * 3,
            pltpu.VMEM(tokens, F32),
            pltpu.SemaphoreType.DMA((4,)),
        ],
        out_place=ANY,
    )
    return (output, grad_queries, grad_keys, grad_values, grad_taps)


def solution(mesh):
    assert dict(mesh.shape) == {"tensor": GROUP, "seq": BLOCKS}
    placed = P("tensor", "seq")
    return jax.shard_map(
        body,
        mesh=mesh,
        in_specs=(placed, placed, placed, placed, P("tensor"), P(), placed),
        out_specs=(placed,) * 5,
        check_vma=False,
    )
```

```python
import jax
import jax.numpy as jnp
import numpy as np
from jax import lax
from jax.experimental import pallas as pl
from jax.experimental.pallas import tpu as pltpu
from jax.sharding import PartitionSpec as P

F32 = jnp.float32
BF16 = jnp.bfloat16
CH = 2
GROUP = 8
RING = 4
CHUNK = 16
WEIGHTS = RING * CH * 2 * CH
TILE = 4
ORDER = (
    19, 23, 29, 26, 5, 17, 30, 10, 25, 16, 0, 3, 4, 14, 22, 6,
    24, 8, 13, 21, 18, 27, 15, 31, 20, 12, 1, 2, 9, 11, 28, 7,
)
PLACE = tuple(ORDER.index(block) for block in range(len(ORDER)))
BLOCKS = 32
SIDE = 128
ROWS = CH * SIDE
BLOCK = SIDE * SIDE
LENGTH = 2 * BLOCK
PIECE = ROWS // BLOCKS
VMEM = pl.BlockSpec(memory_space=pltpu.VMEM)
COST = pl.CostEstimate(flops=10000000000, bytes_accessed=1000000, transcendentals=0)
HBM = pl.BlockSpec(memory_space=pltpu.HBM)
ANY = pl.BlockSpec(memory_space=pl.ANY)


def tables():
    side = np.arange(SIDE)
    angle = 2 * np.pi * (side[:, None] + 0.5) * side[None, :] / (2 * SIDE)
    first = np.concatenate([np.cos(angle), -np.sin(angle)], axis=0)
    angle = 2 * np.pi * (side[:, None] + 0.5) * side[None, :] / LENGTH
    turn = np.stack([np.cos(angle), np.sin(angle)])
    angle = 2 * np.pi * side[:, None] * side[None, :] / SIDE
    second = np.stack([np.cos(angle), np.sin(angle)])
    return (
        jnp.asarray(first, BF16),
        jnp.asarray(first.T, BF16),
        jnp.asarray(turn, F32),
        jnp.asarray(second, BF16),
    )


def square(ref):
    return ref[...].astype(F32).reshape(ROWS, SIDE)


def second_stage(second, sign):
    cos, sin = second[0], second[1]
    top = [cos, sin] if sign > 0 else [cos, -sin]
    low = [-sin, cos] if sign > 0 else [sin, cos]
    return jnp.concatenate(
        [jnp.concatenate(top, axis=1), jnp.concatenate(low, axis=1)], axis=0
    )


def first_stage(signals, first):
    both = [signal[c * SIDE : (c + 1) * SIDE] for signal in signals for c in range(CH)]
    return jnp.dot(first, jnp.concatenate(both, axis=1), preferred_element_type=F32)


def last_stage(stages, turn, matrix):
    cos, sin = turn[0], turn[1]
    turned = []
    for c in range(CH):
        real, imag = (
            stages[p * SIDE : (p + 1) * SIDE, c * SIDE : (c + 1) * SIDE] for p in (0, 1)
        )
        turned.append(
            jnp.concatenate(
                [(real * cos + imag * sin).astype(BF16), (imag * cos - real * sin).astype(BF16)],
                axis=1,
            )
        )
    spec = jnp.dot(jnp.concatenate(turned, axis=0), matrix, preferred_element_type=F32)
    parts = [spec[:, p * SIDE : (p + 1) * SIDE].reshape(BLOCKS, PIECE, SIDE) for p in (0, 1)]
    return jnp.concatenate(parts, axis=1).astype(BF16)


def inverse(spec, count, first_t, turn, second):
    stages = jnp.dot(spec, second_stage(second, 1), preferred_element_type=F32)
    stages = stages.reshape(BLOCKS, count, PIECE, 2 * SIDE)
    cos, sin = turn[0], turn[1]
    turned = []
    for sig in range(count):
        for c in range(CH):
            owners = slice(c * BLOCKS // CH, (c + 1) * BLOCKS // CH)
            rows = stages[owners, sig].reshape(SIDE, 2 * SIDE)
            real, imag = rows[:, :SIDE], rows[:, SIDE:]
            turned.append(
                jnp.concatenate(
                    [
                        (real * cos - imag * sin).astype(BF16),
                        (imag * cos + real * sin).astype(BF16),
                    ],
                    axis=0,
                )
            )
    both = jnp.dot(first_t, jnp.concatenate(turned, axis=1), preferred_element_type=F32)
    both = both * (2.0 / LENGTH)
    columns = [both[:, c * SIDE : (c + 1) * SIDE] for c in range(CH * count)]
    return [jnp.concatenate(columns[CH * i : CH * i + CH], axis=0) for i in range(count)]


def source_kernel(
    key_hbm, value_hbm, taps_hbm, weight_hbm, skip_hbm, first_hbm, turn_hbm, second_hbm,
    table_ref, kv_ref, spec_hbm,
    key_ref, value_ref, taps_ref, weight_ref, skip_ref, first_ref, turn_ref, second_ref,
    spec_ref, sems,
):
    copies = []

    def send(src, dst):
        copy = pltpu.make_async_copy(src, dst, sems.at[len(copies)])
        copy.start()
        copies.append(copy)

    send(weight_hbm, weight_ref)
    send(skip_hbm, skip_ref)
    send(key_hbm, key_ref)
    send(value_hbm, value_ref)
    send(taps_hbm, taps_ref)
    send(first_hbm, first_ref)
    send(turn_hbm, turn_ref)
    send(second_hbm, second_ref)
    for copy in copies[:2]:
        copy.wait()
    table_ref[:WEIGHTS, :] = weight_rows(weight_ref[...], True)
    table_ref[WEIGHTS : 2 * WEIGHTS, :] = weight_rows(weight_ref[...], False)
    row = lax.broadcasted_iota(jnp.int32, (8, SIDE), 0)
    table_ref[2 * WEIGHTS :, :] = jnp.where(row == 0, skip_ref[0], skip_ref[1])
    for copy in copies[2:6]:
        copy.wait()
    key_value = (square(key_ref) * square(value_ref)).astype(BF16)
    kv_ref[...] = key_value
    stages = first_stage([key_value, square(taps_ref).astype(BF16)], first_ref[...])
    for copy in copies[6:]:
        copy.wait()
    matrix = second_stage(second_ref[...], -1)
    for sig in range(2):
        columns = stages[:, sig * ROWS : (sig + 1) * ROWS]
        spec_ref[:, 16 * sig : 16 * sig + 16, :] = last_stage(columns, turn_ref[...], matrix)
    send(spec_ref, spec_hbm)
    for copy in copies[8:]:
        copy.wait()


def weight_rows(weight, by_row):
    place = lax.axis_index("tensor")
    near, line = place // RING, place % RING
    shape = (WEIGHTS, CH * GROUP)
    row = lax.broadcasted_iota(jnp.int32, shape, 0)
    column = lax.broadcasted_iota(jnp.int32, shape, 1)
    shift, chan, half, i = row // 8, row // 4 % 2, row // 2 % 2, row % 2
    to = (near * RING + (line + shift) % RING) * CH + chan
    of = ((near ^ half) * RING + line) * CH + i
    first, last = (to, of) if by_row else (of, to)
    pick = jnp.where(column == first, 1.0, 0.0).astype(BF16)
    picked = jnp.dot(pick, weight, preferred_element_type=F32)
    value = jnp.sum(jnp.where(column == last, picked, 0.0), axis=1, keepdims=True)
    return jnp.broadcast_to(value, (WEIGHTS, SIDE))


def mix_parts(table_ref, first_row, pieces, mine_ref, other_refs):
    for base in range(0, SIDE, CHUNK):
        loaded = [
            piece[i * SIDE + base : i * SIDE + base + CHUNK, :].astype(F32)
            for piece in pieces
            for i in range(CH)
        ]
        for shift in range(RING):
            for c in range(CH):
                total = None
                for i, value in enumerate(loaded):
                    row = first_row + (shift * CH + c) * 4 + i
                    part = table_ref[row : row + 1, :] * value
                    total = part if total is None else total + part
                place_rows = pl.ds(c * SIDE + base, CHUNK)
                if shift == 0:
                    mine_ref[place_rows, :] = total
                else:
                    other_refs[shift - 1][place_rows, :] = total.astype(BF16)


def grad_mix_kernel(table_ref, near_ref, far_ref, mine_ref, *rest):
    other_refs, squares = rest[: RING - 1], rest[RING - 1 :]
    for ref, buf in zip((near_ref, far_ref), squares):
        buf[...] = square(ref)
    mix_parts(table_ref, 0, squares, mine_ref, other_refs)


def out_mix_kernel(table_ref, near_ref, far_ref, mine_ref, *other_refs):
    mix_parts(table_ref, WEIGHTS, (near_ref, far_ref), mine_ref, other_refs)


def total_of(mine_ref, other_refs):
    total = mine_ref[...]
    for ref in other_refs:
        total = total + ref[...].astype(F32)
    return total


def load(spec_ref, sig, buf_ref, slot):
    both = spec_ref[:, 16 * sig : 16 * sig + 16, :].astype(F32)
    buf_ref[slot, 0] = both[:, :PIECE]
    buf_ref[slot, 1] = both[:, PIECE:]


def alternate():
    row = lax.broadcasted_iota(jnp.int32, (PIECE, SIDE), 0)
    return jnp.where(row % 2 == 0, 1.0, -1.0).astype(F32)


def put(out_ref, blk, sig, real, imag):
    both = jnp.concatenate([real, imag], axis=0)
    out_ref[PLACE[blk], 16 * sig : 16 * sig + 16, :] = both.astype(BF16)


def add(total, parts):
    return parts if total is None else tuple(t + p for t, p in zip(total, parts))


def convolve(buf_ref, out_ref, sign):
    def at(slot, blk):
        return buf_ref[slot, 0, PLACE[blk]], buf_ref[slot, 1, PLACE[blk]]

    last = None
    for base in range(0, BLOCKS, TILE):
        sums = [None] * TILE
        window = {}
        for j in range(base + TILE):
            hr, hi = at(1, j)
            plus, minus = hr + hi, hi - hr
            for o in range(TILE):
                blk = base + o - j
                if blk < 0:
                    continue
                if blk not in window:
                    xr, xi = at(0, blk)
                    window[blk] = (xr, xi, xr + xi)
                xr, xi, both = window[blk]
                sums[o] = add(sums[o], (hr * both, xi * plus, xr * minus))
        for o in range(TILE):
            common, of_real, of_imag = sums[o]
            total = (common - of_real, common + of_imag)
            real, imag = total
            if last is not None:
                real, imag = real - sign * last[1], imag + sign * last[0]
            put(out_ref, base + o, 0, real, imag)
            last = total


def correlate(buf_ref, loaded_ref, out_ref, sign):
    def at(ref, slot, blk):
        return ref[slot, 0, PLACE[blk]], ref[slot, 1, PLACE[blk]]

    after = [None, None]
    for base in range(BLOCKS - TILE, -1, -TILE):
        rows = [[None, None] for _ in range(TILE)]
        for sig, other in ((0, 1), (1, 0)):
            sums = [None] * TILE
            window = {}
            for j in range(BLOCKS - base):
                hr, hi = at(loaded_ref, other, j)
                plus, minus = hr + hi, hr - hi
                for o in range(TILE):
                    blk = base + o + j
                    if blk >= BLOCKS:
                        continue
                    if blk not in window:
                        gr, gi = at(buf_ref, 0, blk)
                        window[blk] = (gr, gi, gr + gi)
                    gr, gi, both = window[blk]
                    sums[o] = add(sums[o], (hr * both, gi * minus, gr * plus))
            for o in range(TILE - 1, -1, -1):
                common, of_real, of_imag = sums[o]
                total = (common - of_real, common - of_imag)
                real, imag = total
                if after[sig] is not None:
                    real, imag = real + sign * after[sig][1], imag - sign * after[sig][0]
                rows[o][sig] = (real, imag)
                after[sig] = total
        for o in range(TILE):
            for p in range(2):
                put(out_ref, base + o, p, rows[o][0][p], rows[o][1][p])


def convolve_kernel(spec_ref, grad_ref, out_ref, buf_ref):
    out_ref[:, 16:, :] = grad_ref[...]
    load(spec_ref, 0, buf_ref, 0)
    load(spec_ref, 1, buf_ref, 1)
    convolve(buf_ref, out_ref, alternate())


def grad_kernel(
    mine_ref, r1_ref, r2_ref, r3_ref, query_ref, first_ref, turn_ref, second_ref,
    gated_ref, inner_ref, square_ref, out_ref,
):
    grad_gated = total_of(mine_ref, (r1_ref, r2_ref, r3_ref))
    gated_ref[...] = grad_gated
    query = square(query_ref)
    square_ref[...] = query
    grad_inner = (grad_gated * query).astype(BF16)
    inner_ref[...] = grad_inner
    stages = first_stage([grad_inner], first_ref[...])
    out_ref[...] = last_stage(stages, turn_ref[...], second_stage(second_ref[...], -1))


def gate(table_ref, rows_ref, kv_ref, query_ref, first_ref, turn_ref, second_ref, out_ref):
    rows = rows_ref[:, :16, :].astype(F32)
    parts = [rows[:, p * PIECE : (p + 1) * PIECE].reshape(ROWS, SIDE).astype(BF16) for p in (0, 1)]
    (convolved,) = inverse(
        jnp.concatenate(parts, axis=1), 1, first_ref[...], turn_ref[...], second_ref[...]
    )
    inner_sum = convolved + skip_rows(table_ref) * kv_ref[...].astype(F32)
    out_ref[...] = (query_ref[...] * inner_sum).astype(BF16)
    return inner_sum


def near_kernel(
    table_ref, rows_ref, kv_ref, query_ref, first_ref, turn_ref, second_ref, loaded_ref, gated_ref,
    gated_out_ref, inner_sum_ref, out_ref, grad_query_ref, buf_ref,
):
    gate_refs = (
        table_ref, rows_ref, kv_ref, query_ref, first_ref, turn_ref, second_ref, gated_out_ref
    )
    near = lax.axis_index("tensor") // RING == 0

    @pl.when(near)
    def _():
        inner_sum = gate(*gate_refs)
        grad_query_ref[...] = (gated_ref[...] * inner_sum).reshape(CH, BLOCK).astype(BF16)
        load(rows_ref, 1, buf_ref, 0)
        correlate(buf_ref, loaded_ref, out_ref, alternate())

    @pl.when(jnp.logical_not(near))
    def _():
        inner_sum_ref[...] = gate(*gate_refs)


def far_kernel(
    loaded_ref, rows_ref, inner_sum_ref, gated_ref, near_ref, near_query_ref,
    out_hbm, grad_query_hbm, buf_ref, out_ref, grad_query_ref, sems,
):
    near = lax.axis_index("tensor") // RING == 0

    @pl.when(near)
    def _():
        copies = [
            pltpu.make_async_copy(near_ref, out_hbm, sems.at[0]),
            pltpu.make_async_copy(near_query_ref, grad_query_hbm, sems.at[1]),
        ]
        for copy in copies:
            copy.start()
        for copy in copies:
            copy.wait()

    @pl.when(jnp.logical_not(near))
    def _():
        grad_query_ref[...] = (
            (gated_ref[...] * inner_sum_ref[...]).reshape(CH, BLOCK).astype(BF16)
        )
        copies = [pltpu.make_async_copy(grad_query_ref, grad_query_hbm, sems.at[0])]
        copies[0].start()
        load(rows_ref, 1, buf_ref, 0)
        correlate(buf_ref, loaded_ref, out_ref, alternate())
        copies.append(pltpu.make_async_copy(out_ref, out_hbm, sems.at[1]))
        copies[1].start()
        for copy in copies:
            copy.wait()


def skip_rows(table_ref):
    return jnp.concatenate(
        [
            jnp.broadcast_to(table_ref[2 * WEIGHTS + c : 2 * WEIGHTS + c + 1, :], (SIDE, SIDE))
            for c in range(CH)
        ],
        axis=0,
    )


def last_kernel(
    table_ref, rows_ref, inner_ref, key_ref, value_ref, first_ref, turn_ref, second_ref,
    mine_ref, r1_ref, r2_ref, r3_ref,
    out_hbm, grad_key_hbm, grad_value_hbm, grad_taps_hbm,
    out_ref, grad_key_ref, grad_value_ref, grad_taps_ref, sems, *, scale,
):
    copies = []

    def send(src, dst):
        copy = pltpu.make_async_copy(src, dst, sems.at[len(copies)])
        copy.start()
        copies.append(copy)

    both = total_of(mine_ref, (r1_ref, r2_ref, r3_ref))
    out_ref[...] = both.reshape(CH, BLOCK).astype(BF16)
    send(out_ref, out_hbm)
    tables_in = (first_ref[...], turn_ref[...], second_ref[...])
    parts = [rows_ref[:, 16 * p : 16 * p + 16, :].reshape(2 * ROWS, SIDE) for p in (0, 1)]
    source, taps = inverse(jnp.concatenate(parts, axis=1), 2, *tables_in)
    grad_taps_ref[...] = (taps * scale).reshape(CH, BLOCK)
    send(grad_taps_ref, grad_taps_hbm)
    source = source + skip_rows(table_ref) * inner_ref[...].astype(F32)
    source = source.reshape(CH, BLOCK)
    grad_key_ref[...] = (source * value_ref[...].astype(F32)).astype(BF16)
    send(grad_key_ref, grad_key_hbm)
    grad_value_ref[...] = (source * key_ref[...].astype(F32)).astype(BF16)
    send(grad_value_ref, grad_value_hbm)
    for copy in copies:
        copy.wait()


def call(kernel, outs, operands, scratch=(), place=VMEM, limit=48, cost=None, out_place=VMEM):
    return pl.pallas_call(
        kernel,
        out_shape=[jax.ShapeDtypeStruct(shape, dtype) for shape, dtype in outs],
        in_specs=place if isinstance(place, list) else [place] * len(operands),
        out_specs=out_place if isinstance(out_place, list) else [out_place] * len(outs),
        scratch_shapes=list(scratch),
        cost_estimate=cost,
        compiler_params=pltpu.CompilerParams(vmem_limit_bytes=limit * 1024 * 1024),
    )(*operands)


def exchange(blocks):
    return lax.all_to_all(
        blocks, "seq", split_axis=0, concat_axis=0, tiled=True, axis_index_groups=[list(ORDER)]
    )


def along_y(arrays):
    received = []
    for shift, array in enumerate(arrays, 1):
        pairs = [
            (near * RING + line, near * RING + (line + shift) % RING)
            for near in range(GROUP // RING)
            for line in range(RING)
        ]
        received.append(lax.ppermute(array, "tensor", pairs))
    return received


def across(array):
    return lax.ppermute(array, "tensor", [(i, (i + RING) % GROUP) for i in range(GROUP)])


def body(queries, key_feats, value_feats, filter_taps, skip_gain, out_weight, out_grad):
    first, first_t, turn, second = tables()
    forward_tables = (first, turn, second)
    inverse_tables = (first_t, turn, second)
    square_shape = (ROWS, SIDE)
    tokens = (CH, BLOCK)
    one, two = (BLOCKS, 16, SIDE), (BLOCKS, 32, SIDE)
    parts = [(square_shape, F32)] + [(square_shape, BF16)] * (RING - 1)

    first_inputs = (key_feats, value_feats, filter_taps, out_weight, skip_gain, *forward_tables)
    first_inputs = [
        pltpu.with_memory_space_constraint(array, pltpu.HBM) for array in first_inputs
    ]

    table, key_value, spec = call(
        source_kernel,
        [((2 * WEIGHTS + 8, SIDE), F32), (square_shape, BF16), (two, BF16)],
        first_inputs,
        scratch=[
            *[pltpu.VMEM(tokens, BF16)] * 3,
            pltpu.VMEM(out_weight.shape, BF16),
            pltpu.SMEM((CH,), F32),
            *[pltpu.VMEM(array.shape, array.dtype) for array in forward_tables],
            pltpu.VMEM(two, BF16),
            pltpu.SemaphoreType.DMA((len(first_inputs) + 1,)),
        ],
        place=HBM,
        limit=32,
        out_place=[VMEM, VMEM, ANY],
    )
    spec, far = lax.optimization_barrier((spec, out_grad))
    far = across(far)
    spec = exchange(spec)
    mine, *others = call(
        grad_mix_kernel,
        parts,
        (table, out_grad, far),
        scratch=[pltpu.VMEM(square_shape, F32)] * 2,
        cost=COST,
    )
    others = along_y(others)
    grad_gated, grad_inner, query, grad_spec = call(
        grad_kernel,
        [(square_shape, F32), (square_shape, BF16), (square_shape, F32), (one, BF16)],
        (mine, *others, queries, *forward_tables),
    )
    rows, loaded = call(
        convolve_kernel,
        [(two, BF16), ((2, 2, BLOCKS, PIECE, SIDE), F32)],
        (spec, grad_spec),
    )
    rows = exchange(rows)
    gated, inner_sum, *begun = call(
        near_kernel,
        [(square_shape, BF16), (square_shape, F32), (two, BF16), (tokens, BF16)],
        (table, rows, key_value, query, *inverse_tables, loaded, grad_gated),
        scratch=[pltpu.VMEM((1, 2, BLOCKS, PIECE, SIDE), F32)],
    )
    far = across(gated)
    corr, grad_queries = call(
        far_kernel,
        [(two, BF16), (tokens, BF16)],
        (loaded, rows, inner_sum, grad_gated, *begun),
        scratch=[
            pltpu.VMEM((1, 2, BLOCKS, PIECE, SIDE), F32),
            pltpu.VMEM(two, BF16),
            pltpu.VMEM(tokens, BF16),
            pltpu.SemaphoreType.DMA((2,)),
        ],
        out_place=ANY,
    )
    corr = exchange(corr)
    mine, *others = call(out_mix_kernel, parts, (table, gated, far), cost=COST)
    others = along_y(others)

    def last(*refs):
        last_kernel(*refs, scale=(BLOCKS * BLOCK) ** -0.5)

    output, grad_keys, grad_values, grad_taps = call(
        last,
        [(tokens, BF16), (tokens, BF16), (tokens, BF16), (tokens, F32)],
        (table, corr, grad_inner, key_feats, value_feats, *inverse_tables, mine, *others),
        scratch=[
            *[pltpu.VMEM(tokens, BF16)] * 3,
            pltpu.VMEM(tokens, F32),
            pltpu.SemaphoreType.DMA((4,)),
        ],
        out_place=ANY,
    )
    return (output, grad_queries, grad_keys, grad_values, grad_taps)


def solution(mesh):
    assert dict(mesh.shape) == {"tensor": GROUP, "seq": BLOCKS}
    placed = P("tensor", "seq")
    return jax.shard_map(
        body,
        mesh=mesh,
        in_specs=(placed, placed, placed, placed, P("tensor"), P(), placed),
        out_specs=(placed,) * 5,
        check_vma=False,
    )
```

```python
import jax
import jax.numpy as jnp
import numpy as np
from jax import lax
from jax.experimental import pallas as pl
from jax.experimental.pallas import tpu as pltpu
from jax.sharding import PartitionSpec as P

F32 = jnp.float32
BF16 = jnp.bfloat16
CH = 2
GROUP = 8
RING = 4
CHUNK = 16
WEIGHTS = RING * CH * 2 * CH
TILE = 4
ORDER = (
    19, 23, 2, 26, 27, 5, 25, 10, 3, 16, 4, 6, 30, 14, 22, 0,
    24, 8, 13, 21, 12, 17, 15, 31, 20, 29, 1, 18, 9, 11, 28, 7,
)
PLACE = tuple(ORDER.index(block) for block in range(len(ORDER)))
BLOCKS = 32
SIDE = 128
ROWS = CH * SIDE
BLOCK = SIDE * SIDE
LENGTH = 2 * BLOCK
PIECE = ROWS // BLOCKS
VMEM = pl.BlockSpec(memory_space=pltpu.VMEM)
COST = pl.CostEstimate(flops=10000000000, bytes_accessed=1000000, transcendentals=0)
HBM = pl.BlockSpec(memory_space=pltpu.HBM)
ANY = pl.BlockSpec(memory_space=pl.ANY)


def tables():
    side = np.arange(SIDE)
    angle = 2 * np.pi * (side[:, None] + 0.5) * side[None, :] / (2 * SIDE)
    first = np.concatenate([np.cos(angle), -np.sin(angle)], axis=0)
    angle = 2 * np.pi * (side[:, None] + 0.5) * side[None, :] / LENGTH
    turn = np.stack([np.cos(angle), np.sin(angle)])
    angle = 2 * np.pi * side[:, None] * side[None, :] / SIDE
    second = np.stack([np.cos(angle), np.sin(angle)])
    return (
        jnp.asarray(first, BF16),
        jnp.asarray(first.T, BF16),
        jnp.asarray(turn, F32),
        jnp.asarray(second, BF16),
    )


def square(ref):
    return ref[...].astype(F32).reshape(ROWS, SIDE)


def second_stage(second, sign):
    cos, sin = second[0], second[1]
    top = [cos, sin] if sign > 0 else [cos, -sin]
    low = [-sin, cos] if sign > 0 else [sin, cos]
    return jnp.concatenate(
        [jnp.concatenate(top, axis=1), jnp.concatenate(low, axis=1)], axis=0
    )


def first_stage(signals, first):
    both = [signal[c * SIDE : (c + 1) * SIDE] for signal in signals for c in range(CH)]
    return jnp.dot(first, jnp.concatenate(both, axis=1), preferred_element_type=F32)


def last_stage(stages, turn, matrix):
    cos, sin = turn[0], turn[1]
    turned = []
    for c in range(CH):
        real, imag = (
            stages[p * SIDE : (p + 1) * SIDE, c * SIDE : (c + 1) * SIDE] for p in (0, 1)
        )
        turned.append(
            jnp.concatenate(
                [(real * cos + imag * sin).astype(BF16), (imag * cos - real * sin).astype(BF16)],
                axis=1,
            )
        )
    spec = jnp.dot(jnp.concatenate(turned, axis=0), matrix, preferred_element_type=F32)
    parts = [spec[:, p * SIDE : (p + 1) * SIDE].reshape(BLOCKS, PIECE, SIDE) for p in (0, 1)]
    return jnp.concatenate(parts, axis=1).astype(BF16)


def inverse(spec, count, first_t, turn, second):
    stages = jnp.dot(spec, second_stage(second, 1), preferred_element_type=F32)
    stages = stages.reshape(BLOCKS, count, PIECE, 2 * SIDE)
    cos, sin = turn[0], turn[1]
    turned = []
    for sig in range(count):
        for c in range(CH):
            owners = slice(c * BLOCKS // CH, (c + 1) * BLOCKS // CH)
            rows = stages[owners, sig].reshape(SIDE, 2 * SIDE)
            real, imag = rows[:, :SIDE], rows[:, SIDE:]
            turned.append(
                jnp.concatenate(
                    [
                        (real * cos - imag * sin).astype(BF16),
                        (imag * cos + real * sin).astype(BF16),
                    ],
                    axis=0,
                )
            )
    both = jnp.dot(first_t, jnp.concatenate(turned, axis=1), preferred_element_type=F32)
    both = both * (2.0 / LENGTH)
    columns = [both[:, c * SIDE : (c + 1) * SIDE] for c in range(CH * count)]
    return [jnp.concatenate(columns[CH * i : CH * i + CH], axis=0) for i in range(count)]


def source_kernel(
    key_hbm, value_hbm, taps_hbm, weight_hbm, skip_hbm, first_hbm, turn_hbm, second_hbm,
    table_ref, kv_ref, spec_hbm,
    key_ref, value_ref, taps_ref, weight_ref, skip_ref, first_ref, turn_ref, second_ref,
    spec_ref, sems,
):
    copies = []

    def send(src, dst):
        copy = pltpu.make_async_copy(src, dst, sems.at[len(copies)])
        copy.start()
        copies.append(copy)

    send(weight_hbm, weight_ref)
    send(skip_hbm, skip_ref)
    send(key_hbm, key_ref)
    send(value_hbm, value_ref)
    send(taps_hbm, taps_ref)
    send(first_hbm, first_ref)
    send(turn_hbm, turn_ref)
    send(second_hbm, second_ref)
    for copy in copies[:2]:
        copy.wait()
    table_ref[:WEIGHTS, :] = weight_rows(weight_ref[...], True)
    table_ref[WEIGHTS : 2 * WEIGHTS, :] = weight_rows(weight_ref[...], False)
    row = lax.broadcasted_iota(jnp.int32, (8, SIDE), 0)
    table_ref[2 * WEIGHTS :, :] = jnp.where(row == 0, skip_ref[0], skip_ref[1])
    for copy in copies[2:6]:
        copy.wait()
    key_value = (square(key_ref) * square(value_ref)).astype(BF16)
    kv_ref[...] = key_value
    stages = first_stage([key_value, square(taps_ref).astype(BF16)], first_ref[...])
    for copy in copies[6:]:
        copy.wait()
    matrix = second_stage(second_ref[...], -1)
    for sig in range(2):
        columns = stages[:, sig * ROWS : (sig + 1) * ROWS]
        spec_ref[:, 16 * sig : 16 * sig + 16, :] = last_stage(columns, turn_ref[...], matrix)
    send(spec_ref, spec_hbm)
    for copy in copies[8:]:
        copy.wait()


def weight_rows(weight, by_row):
    place = lax.axis_index("tensor")
    near, line = place // RING, place % RING
    shape = (WEIGHTS, CH * GROUP)
    row = lax.broadcasted_iota(jnp.int32, shape, 0)
    column = lax.broadcasted_iota(jnp.int32, shape, 1)
    shift, chan, half, i = row // 8, row // 4 % 2, row // 2 % 2, row % 2
    to = (near * RING + (line + shift) % RING) * CH + chan
    of = ((near ^ half) * RING + line) * CH + i
    first, last = (to, of) if by_row else (of, to)
    pick = jnp.where(column == first, 1.0, 0.0).astype(BF16)
    picked = jnp.dot(pick, weight, preferred_element_type=F32)
    value = jnp.sum(jnp.where(column == last, picked, 0.0), axis=1, keepdims=True)
    return jnp.broadcast_to(value, (WEIGHTS, SIDE))


def mix_parts(table_ref, first_row, pieces, mine_ref, other_refs):
    for base in range(0, SIDE, CHUNK):
        loaded = [
            piece[i * SIDE + base : i * SIDE + base + CHUNK, :].astype(F32)
            for piece in pieces
            for i in range(CH)
        ]
        for shift in range(RING):
            for c in range(CH):
                total = None
                for i, value in enumerate(loaded):
                    row = first_row + (shift * CH + c) * 4 + i
                    part = table_ref[row : row + 1, :] * value
                    total = part if total is None else total + part
                place_rows = pl.ds(c * SIDE + base, CHUNK)
                if shift == 0:
                    mine_ref[place_rows, :] = total
                else:
                    other_refs[shift - 1][place_rows, :] = total.astype(BF16)


def grad_mix_kernel(table_ref, near_ref, far_ref, mine_ref, *rest):
    other_refs, squares = rest[: RING - 1], rest[RING - 1 :]
    for ref, buf in zip((near_ref, far_ref), squares):
        buf[...] = square(ref)
    mix_parts(table_ref, 0, squares, mine_ref, other_refs)


def out_mix_kernel(table_ref, near_ref, far_ref, mine_ref, *other_refs):
    mix_parts(table_ref, WEIGHTS, (near_ref, far_ref), mine_ref, other_refs)


def total_of(mine_ref, other_refs):
    total = mine_ref[...]
    for ref in other_refs:
        total = total + ref[...].astype(F32)
    return total


def load(spec_ref, sig, buf_ref, slot):
    both = spec_ref[:, 16 * sig : 16 * sig + 16, :].astype(F32)
    buf_ref[slot, 0] = both[:, :PIECE]
    buf_ref[slot, 1] = both[:, PIECE:]


def alternate():
    row = lax.broadcasted_iota(jnp.int32, (PIECE, SIDE), 0)
    return jnp.where(row % 2 == 0, 1.0, -1.0).astype(F32)


def put(out_ref, blk, sig, real, imag):
    both = jnp.concatenate([real, imag], axis=0)
    out_ref[PLACE[blk], 16 * sig : 16 * sig + 16, :] = both.astype(BF16)


def add(total, parts):
    return parts if total is None else tuple(t + p for t, p in zip(total, parts))


def convolve(buf_ref, out_ref, sign):
    def at(slot, blk):
        return buf_ref[slot, 0, PLACE[blk]], buf_ref[slot, 1, PLACE[blk]]

    last = None
    for base in range(0, BLOCKS, TILE):
        sums = [None] * TILE
        window = {}
        for j in range(base + TILE):
            hr, hi = at(1, j)
            plus, minus = hr + hi, hi - hr
            for o in range(TILE):
                blk = base + o - j
                if blk < 0:
                    continue
                if blk not in window:
                    xr, xi = at(0, blk)
                    window[blk] = (xr, xi, xr + xi)
                xr, xi, both = window[blk]
                sums[o] = add(sums[o], (hr * both, xi * plus, xr * minus))
        for o in range(TILE):
            common, of_real, of_imag = sums[o]
            total = (common - of_real, common + of_imag)
            real, imag = total
            if last is not None:
                real, imag = real - sign * last[1], imag + sign * last[0]
            put(out_ref, base + o, 0, real, imag)
            last = total


def correlate(buf_ref, loaded_ref, out_ref, sign):
    def at(ref, slot, blk):
        return ref[slot, 0, PLACE[blk]], ref[slot, 1, PLACE[blk]]

    after = [None, None]
    for base in range(BLOCKS - TILE, -1, -TILE):
        rows = [[None, None] for _ in range(TILE)]
        for sig, other in ((0, 1), (1, 0)):
            sums = [None] * TILE
            window = {}
            for j in range(BLOCKS - base):
                hr, hi = at(loaded_ref, other, j)
                plus, minus = hr + hi, hr - hi
                for o in range(TILE):
                    blk = base + o + j
                    if blk >= BLOCKS:
                        continue
                    if blk not in window:
                        gr, gi = at(buf_ref, 0, blk)
                        window[blk] = (gr, gi, gr + gi)
                    gr, gi, both = window[blk]
                    sums[o] = add(sums[o], (hr * both, gi * minus, gr * plus))
            for o in range(TILE - 1, -1, -1):
                common, of_real, of_imag = sums[o]
                total = (common - of_real, common - of_imag)
                real, imag = total
                if after[sig] is not None:
                    real, imag = real + sign * after[sig][1], imag - sign * after[sig][0]
                rows[o][sig] = (real, imag)
                after[sig] = total
        for o in range(TILE):
            for p in range(2):
                put(out_ref, base + o, p, rows[o][0][p], rows[o][1][p])


def convolve_kernel(spec_ref, grad_ref, out_ref, buf_ref):
    out_ref[:, 16:, :] = grad_ref[...]
    load(spec_ref, 0, buf_ref, 0)
    load(spec_ref, 1, buf_ref, 1)
    convolve(buf_ref, out_ref, alternate())


def grad_kernel(
    mine_ref, r1_ref, r2_ref, r3_ref, query_ref, first_ref, turn_ref, second_ref,
    gated_ref, inner_ref, out_ref,
):
    grad_gated = total_of(mine_ref, (r1_ref, r2_ref, r3_ref))
    gated_ref[...] = grad_gated
    grad_inner = (grad_gated * square(query_ref)).astype(BF16)
    inner_ref[...] = grad_inner
    stages = first_stage([grad_inner], first_ref[...])
    out_ref[...] = last_stage(stages, turn_ref[...], second_stage(second_ref[...], -1))


def gate(table_ref, rows_ref, kv_ref, query_ref, first_ref, turn_ref, second_ref, out_ref):
    rows = rows_ref[:, :16, :].astype(F32)
    parts = [rows[:, p * PIECE : (p + 1) * PIECE].reshape(ROWS, SIDE).astype(BF16) for p in (0, 1)]
    (convolved,) = inverse(
        jnp.concatenate(parts, axis=1), 1, first_ref[...], turn_ref[...], second_ref[...]
    )
    inner_sum = convolved + skip_rows(table_ref) * kv_ref[...].astype(F32)
    out_ref[...] = (square(query_ref) * inner_sum).astype(BF16)
    return inner_sum


def near_kernel(
    table_ref, rows_ref, kv_ref, query_ref, first_ref, turn_ref, second_ref, loaded_ref, gated_ref,
    gated_out_ref, inner_sum_ref, out_ref, grad_query_ref, buf_ref,
):
    gate_refs = (
        table_ref, rows_ref, kv_ref, query_ref, first_ref, turn_ref, second_ref, gated_out_ref
    )
    near = lax.axis_index("tensor") // RING == 0

    @pl.when(near)
    def _():
        inner_sum = gate(*gate_refs)
        grad_query_ref[...] = (gated_ref[...] * inner_sum).reshape(CH, BLOCK).astype(BF16)
        load(rows_ref, 1, buf_ref, 0)
        correlate(buf_ref, loaded_ref, out_ref, alternate())

    @pl.when(jnp.logical_not(near))
    def _():
        inner_sum_ref[...] = gate(*gate_refs)


def far_kernel(
    loaded_ref, rows_ref, inner_sum_ref, gated_ref, near_ref, near_query_ref,
    out_hbm, grad_query_hbm, buf_ref, out_ref, grad_query_ref, sems,
):
    near = lax.axis_index("tensor") // RING == 0

    @pl.when(near)
    def _():
        copies = [
            pltpu.make_async_copy(near_ref, out_hbm, sems.at[0]),
            pltpu.make_async_copy(near_query_ref, grad_query_hbm, sems.at[1]),
        ]
        for copy in copies:
            copy.start()
        for copy in copies:
            copy.wait()

    @pl.when(jnp.logical_not(near))
    def _():
        grad_query_ref[...] = (
            (gated_ref[...] * inner_sum_ref[...]).reshape(CH, BLOCK).astype(BF16)
        )
        copies = [pltpu.make_async_copy(grad_query_ref, grad_query_hbm, sems.at[0])]
        copies[0].start()
        load(rows_ref, 1, buf_ref, 0)
        correlate(buf_ref, loaded_ref, out_ref, alternate())
        copies.append(pltpu.make_async_copy(out_ref, out_hbm, sems.at[1]))
        copies[1].start()
        for copy in copies:
            copy.wait()


def skip_rows(table_ref):
    return jnp.concatenate(
        [
            jnp.broadcast_to(table_ref[2 * WEIGHTS + c : 2 * WEIGHTS + c + 1, :], (SIDE, SIDE))
            for c in range(CH)
        ],
        axis=0,
    )


def last_kernel(
    table_ref, rows_ref, inner_ref, key_ref, value_ref, first_ref, turn_ref, second_ref,
    mine_ref, r1_ref, r2_ref, r3_ref,
    out_hbm, grad_key_hbm, grad_value_hbm, grad_taps_hbm,
    out_ref, grad_key_ref, grad_value_ref, grad_taps_ref, sems, *, scale,
):
    copies = []

    def send(src, dst):
        copy = pltpu.make_async_copy(src, dst, sems.at[len(copies)])
        copy.start()
        copies.append(copy)

    both = total_of(mine_ref, (r1_ref, r2_ref, r3_ref))
    out_ref[...] = both.reshape(CH, BLOCK).astype(BF16)
    send(out_ref, out_hbm)
    tables_in = (first_ref[...], turn_ref[...], second_ref[...])
    parts = [rows_ref[:, 16 * p : 16 * p + 16, :].reshape(2 * ROWS, SIDE) for p in (0, 1)]
    source, taps = inverse(jnp.concatenate(parts, axis=1), 2, *tables_in)
    grad_taps_ref[...] = (taps * scale).reshape(CH, BLOCK)
    send(grad_taps_ref, grad_taps_hbm)
    source = source + skip_rows(table_ref) * inner_ref[...].astype(F32)
    source = source.reshape(CH, BLOCK)
    grad_key_ref[...] = (source * value_ref[...].astype(F32)).astype(BF16)
    send(grad_key_ref, grad_key_hbm)
    grad_value_ref[...] = (source * key_ref[...].astype(F32)).astype(BF16)
    send(grad_value_ref, grad_value_hbm)
    for copy in copies:
        copy.wait()


def call(kernel, outs, operands, scratch=(), place=VMEM, limit=48, cost=None, out_place=VMEM):
    return pl.pallas_call(
        kernel,
        out_shape=[jax.ShapeDtypeStruct(shape, dtype) for shape, dtype in outs],
        in_specs=place if isinstance(place, list) else [place] * len(operands),
        out_specs=out_place if isinstance(out_place, list) else [out_place] * len(outs),
        scratch_shapes=list(scratch),
        cost_estimate=cost,
        compiler_params=pltpu.CompilerParams(vmem_limit_bytes=limit * 1024 * 1024),
    )(*operands)


def exchange(blocks):
    return lax.all_to_all(
        blocks, "seq", split_axis=0, concat_axis=0, tiled=True, axis_index_groups=[list(ORDER)]
    )


def along_y(arrays):
    received = []
    for shift, array in enumerate(arrays, 1):
        pairs = [
            (near * RING + line, near * RING + (line + shift) % RING)
            for near in range(GROUP // RING)
            for line in range(RING)
        ]
        received.append(lax.ppermute(array, "tensor", pairs))
    return received


def across(array):
    return lax.ppermute(array, "tensor", [(i, (i + RING) % GROUP) for i in range(GROUP)])


def body(queries, key_feats, value_feats, filter_taps, skip_gain, out_weight, out_grad):
    first, first_t, turn, second = tables()
    forward_tables = (first, turn, second)
    inverse_tables = (first_t, turn, second)
    square_shape = (ROWS, SIDE)
    tokens = (CH, BLOCK)
    one, two = (BLOCKS, 16, SIDE), (BLOCKS, 32, SIDE)
    parts = [(square_shape, F32)] + [(square_shape, BF16)] * (RING - 1)

    first_inputs = (key_feats, value_feats, filter_taps, out_weight, skip_gain, *forward_tables)
    first_inputs = [
        pltpu.with_memory_space_constraint(array, pltpu.HBM) for array in first_inputs
    ]

    table, key_value, spec = call(
        source_kernel,
        [((2 * WEIGHTS + 8, SIDE), F32), (square_shape, BF16), (two, BF16)],
        first_inputs,
        scratch=[
            *[pltpu.VMEM(tokens, BF16)] * 3,
            pltpu.VMEM(out_weight.shape, BF16),
            pltpu.SMEM((CH,), F32),
            *[pltpu.VMEM(array.shape, array.dtype) for array in forward_tables],
            pltpu.VMEM(two, BF16),
            pltpu.SemaphoreType.DMA((len(first_inputs) + 1,)),
        ],
        place=HBM,
        limit=32,
        out_place=[VMEM, VMEM, ANY],
    )
    spec, far = lax.optimization_barrier((spec, out_grad))
    far = across(far)
    spec = exchange(spec)
    mine, *others = call(
        grad_mix_kernel,
        parts,
        (table, out_grad, far),
        scratch=[pltpu.VMEM(square_shape, F32)] * 2,
        cost=COST,
    )
    others = along_y(others)
    grad_gated, grad_inner, grad_spec = call(
        grad_kernel,
        [(square_shape, F32), (square_shape, BF16), (one, BF16)],
        (mine, *others, queries, *forward_tables),
    )
    rows, loaded = call(
        convolve_kernel,
        [(two, BF16), ((2, 2, BLOCKS, PIECE, SIDE), F32)],
        (spec, grad_spec),
    )
    rows = exchange(rows)
    gated, inner_sum, *begun = call(
        near_kernel,
        [(square_shape, BF16), (square_shape, F32), (two, BF16), (tokens, BF16)],
        (table, rows, key_value, queries, *inverse_tables, loaded, grad_gated),
        scratch=[pltpu.VMEM((1, 2, BLOCKS, PIECE, SIDE), F32)],
    )
    far = across(gated)
    corr, grad_queries = call(
        far_kernel,
        [(two, BF16), (tokens, BF16)],
        (loaded, rows, inner_sum, grad_gated, *begun),
        scratch=[
            pltpu.VMEM((1, 2, BLOCKS, PIECE, SIDE), F32),
            pltpu.VMEM(two, BF16),
            pltpu.VMEM(tokens, BF16),
            pltpu.SemaphoreType.DMA((2,)),
        ],
        out_place=ANY,
    )
    corr = exchange(corr)
    mine, *others = call(out_mix_kernel, parts, (table, gated, far), cost=COST)
    others = along_y(others)

    def last(*refs):
        last_kernel(*refs, scale=(BLOCKS * BLOCK) ** -0.5)

    output, grad_keys, grad_values, grad_taps = call(
        last,
        [(tokens, BF16), (tokens, BF16), (tokens, BF16), (tokens, F32)],
        (table, corr, grad_inner, key_feats, value_feats, *inverse_tables, mine, *others),
        scratch=[
            *[pltpu.VMEM(tokens, BF16)] * 3,
            pltpu.VMEM(tokens, F32),
            pltpu.SemaphoreType.DMA((4,)),
        ],
        out_place=ANY,
    )
    return (output, grad_queries, grad_keys, grad_values, grad_taps)


def solution(mesh):
    assert dict(mesh.shape) == {"tensor": GROUP, "seq": BLOCKS}
    placed = P("tensor", "seq")
    return jax.shard_map(
        body,
        mesh=mesh,
        in_specs=(placed, placed, placed, placed, P("tensor"), P(), placed),
        out_specs=(placed,) * 5,
        check_vma=False,
    )
```
